32 devices in a mesh: ctx: 8 (over y, x, core), chan: 4 (over z).
Axes of the slice: x: 2, y: 2, z: 4, core: 2. Of those that a mesh axis runs over, the one named last changes fastest.
Arguments:
- features: bfloat16 [3, 2048, 4096], P(None, 'ctx', 'chan'), may hold values from -6 to 6
- saved_conv: bfloat16 [2048, 4096], P('ctx', 'chan'), may hold values from -6 to 6
- grad_out: bfloat16 [2048, 4096], P('ctx', 'chan'), may hold values from -6 to 6
- out_weight: bfloat16 [4096, 4096], P('chan'), may hold values from -0.09375 to 0.09375
- in_weight: bfloat16 [3, 4096, 4096], P(None, None, 'chan'), may hold values from -0.09375 to 0.09375
- short_taps: float32 [3, 3, 4096], P(None, None, 'chan'), may hold values from -3.5 to 3.5
- residues: float32 [16, 4096], P(None, 'chan'), may hold values from -1 to 1
- decay_time: float32 [16, 4096], P(None, 'chan'), may hold values from 25 to 10240
Outputs:
- grad_input: bfloat16 [4096, 2048], P('chan', 'ctx')
- grad_residue: float32 [16, 4096], P(None, 'chan')
The draws below stay inside these ranges and needn't reach their ends.
All inputs are finite; a program needn't handle non-finite values.
Results may differ from the reference program's by a relative error of at most 0.019.
Values may be sent and summed in bfloat16 or wider, within the bound.
No kernel may reach another device: no remote copies, remote signals or barrier semaphores. Data moves between devices by JAX's collectives and lax.ppermute only.
A program may use at most 192 MiB of HBM per device.

```python
import jax
import jax.numpy as jnp
from jax import lax

D = 4096
MODES = 16
TAPS = 3
TOKENS = 2048
N_CHAN = 4


def draw_residues(key, part):
    scale = (8.0 * TOKENS) ** (-0.5)
    values = jnp.clip(jax.random.normal(key, (MODES, D), jnp.float32), -6.0, 6.0) * scale
    return values.astype(jnp.float32)


def draw_decay_time(key, part):
    first, second, third = jax.random.split(key, 3)
    share = 0.5
    slow_low = jnp.log(0.5 * TOKENS)
    slow = jnp.exp(jax.random.uniform(first, (MODES, D), jnp.float32, slow_low, jnp.log(5.0 * TOKENS)))
    fast = jnp.exp(jax.random.uniform(second, (MODES, D), jnp.float32, jnp.log(25.0), jnp.log(50.0)))
    pick = jax.random.bernoulli(third, share, (MODES, D))
    return jnp.where(pick, slow, fast).astype(jnp.float32)


def level_of(stream_key, dims, pieces, smallest, high):
    gain = 1.0
    for dim, shards_of in pieces:
        steps = jax.random.uniform(jax.random.fold_in(jax.random.fold_in(stream_key, 6), dim), (shards_of,), jnp.float32, smallest / len(pieces), high / len(pieces))
        gain = gain * jnp.repeat(jnp.exp(steps), dims[dim] // shards_of).reshape((-1,) + (1,) * (len(dims) - 1 - dim))
    return gain


def gaussian(stream_key, dims, width, reach, shards=(), held_as=jnp.bfloat16):
    factor_of = level_of(stream_key, dims, shards, -0.22, 0.18) if shards else 1.0
    values = jax.random.normal(stream_key, dims, jnp.float32) * width * factor_of
    return jnp.minimum(jnp.maximum(values, -reach), reach).astype(held_as)


def setup_inputs(seed: int = 0) -> dict:
    key_list = jax.random.split(jax.random.key(seed), 9)
    features = gaussian(key_list[0], (3, TOKENS, D), 1.0, 6.0, ((1, 8), (2, 4)))
    saved_conv = gaussian(key_list[1], (TOKENS, D), 1.0, 6.0, ((0, 8), (1, 4)))
    grad_out = gaussian(key_list[2], (TOKENS, D), 1.0, 6.0, ((0, 8), (1, 4)))
    out_weight = gaussian(key_list[3], (D, D), D ** -0.5, 0.09375, ((0, 4),))
    in_weight = gaussian(key_list[4], (3, D, D), D ** -0.5, 0.09375, ((2, 4),))
    short_taps = gaussian(key_list[5], (3, TAPS, D), TAPS ** -0.5, 3.5, ((2, 4),), jnp.float32)
    residues = draw_residues(jax.random.fold_in(key_list[8], 71), 0)
    decay_time = draw_decay_time(jax.random.fold_in(key_list[8], 71), 0)
    return {"features": features, "saved_conv": saved_conv, "grad_out": grad_out, "out_weight": out_weight, "in_weight": in_weight, "short_taps": short_taps, "residues": residues, "decay_time": decay_time}


def reference(features, saved_conv, grad_out, out_weight, in_weight, short_taps, residues, decay_time):
    highest = lax.Precision.HIGHEST
    acts = features.astype(jnp.float32)
    query_act = acts[0]
    key_act = acts[1]
    value_act = acts[2]
    grad_gate = jnp.dot(grad_out.astype(jnp.float32), out_weight.astype(jnp.float32).T, precision=highest)
    grad_conv = grad_gate * query_act
    grad_query = grad_gate * saved_conv.astype(jnp.float32)
    product = key_act * value_act
    decay = jnp.exp(-1.0 / decay_time)

    def advance(carry, inputs):
        state, total = carry
        grad_row, prod_row = inputs
        state = grad_row[None, :] + decay * state
        total = total + prod_row[None, :] * state
        return (state, total), jnp.sum(residues * state, axis=0)

    start = (jnp.zeros(residues.shape, jnp.float32), jnp.zeros(residues.shape, jnp.float32))
    (state, total), grad_product = lax.scan(advance, start, (grad_conv, product), reverse=True)
    grad_key = grad_product * value_act
    grad_value = grad_product * key_act
    grad_acts = jnp.stack([grad_query, grad_key, grad_value])
    padded = jnp.pad(grad_acts, ((0, 0), (0, TAPS - 1), (0, 0)))
    filtered = short_taps[:, 0, None, :] * padded[:, 0:TOKENS, :]
    for lag in range(1, TAPS):
        filtered = filtered + short_taps[:, lag, None, :] * padded[:, lag:lag + TOKENS, :]
    grad_proj = filtered.astype(jnp.bfloat16)
    group_width = D // N_CHAN
    accum = jnp.zeros((D, TOKENS), jnp.float32)
    for group in range(N_CHAN):
        low = group * group_width
        high = low + group_width
        term = jnp.zeros((D, TOKENS), jnp.float32)
        for which in range(3):
            term = term + jnp.dot(in_weight[which][:, low:high].astype(jnp.float32), grad_proj[which][:, low:high].astype(jnp.float32).T, precision=highest)
        rounded = lax.optimization_barrier(term.astype(jnp.bfloat16))
        accum = accum + rounded.astype(jnp.float32)
    return accum.astype(jnp.bfloat16), total / TOKENS
```

```python
import functools

import jax
import jax.numpy as jnp
from jax import lax
from jax.experimental import pallas as pl
from jax.experimental.pallas import tpu as pltpu
from jax.sharding import PartitionSpec as P

LANES = 128
ROWS = 8
NT = (((1,), (1,)), ((), ()))


def params(mib):
    return pltpu.CompilerParams(vmem_limit_bytes=mib * 2**20)


def whole(shape):
    return pl.BlockSpec(shape, lambda *_: (0,) * len(shape))


def tile(token):
    return pl.ds(pl.multiple_of(token * ROWS, ROWS), ROWS)


def tree_sum(terms):
    terms = list(terms)
    while len(terms) > 1:
        paired = [a + b for a, b in zip(terms[::2], terms[1::2])]
        terms = paired + terms[2 * len(paired):]
    return terms[0]


def spread_kernel(features, saved, out):
    tokens, width = saved.shape
    if width < ROWS * LANES:
        out[...] = jnp.zeros(out.shape, out.dtype)
    for group in range(width // LANES):
        columns = pl.ds(group * LANES, LANES)
        rows = pl.ds(group, tokens, stride=ROWS)
        for which in range(3):
            out[which, rows, :] = features[which, :, columns].astype(jnp.float32)
        out[3, rows, :] = saved[:, columns].astype(jnp.float32)


def spread_acts(features, saved):
    tokens = saved.shape[0]
    return pl.pallas_call(
        spread_kernel,
        out_shape=jax.ShapeDtypeStruct((4, tokens * ROWS, LANES), jnp.float32),
        compiler_params=params(24),
        name="spread",
    )(features, saved)


def gate_kernel(has_acc, shards, single, scal, *refs):
    acc = refs[0] if has_acc else None
    pieces = refs[has_acc:-1 - shards]
    weights = refs[-1 - shards:-1]
    out = refs[-1]
    half = pieces[0].shape[0]
    for part in range(2):
        rows = pl.ds(part * half, half)
        if single:
            lhs = [jnp.where(scal[shards] > 0, pieces[part][...], pieces[2 + part][...])]
        else:
            lhs = [pieces[2 * shard + part][...] for shard in range(shards)]
        terms = [
            lax.dot_general(x, w[...], NT, preferred_element_type=jnp.float32)
            for x, w in zip(lhs, weights)
        ]
        if has_acc:
            terms.append(acc[rows, :])
        out[rows, :] = tree_sum(terms)


def gate_step(acc, pieces, scalars, weight, shards, single):
    half, deep = pieces[0].shape
    width = weight.shape[0]
    block = min(256, width)
    tokens = 2 * half
    has_acc = acc is not None

    def weight_spec(shard):
        return pl.BlockSpec((block, deep), lambda i, s: (i, s[shard]))

    out_spec = pl.BlockSpec((tokens, block), lambda i, s: (0, i))
    return pl.pallas_call(
        functools.partial(gate_kernel, has_acc, shards, single),
        grid_spec=pltpu.PrefetchScalarGridSpec(
            num_scalar_prefetch=1,
            grid=(width // block,),
            in_specs=([out_spec] if has_acc else [])
            + [whole((half, deep)) for _ in pieces]
            + [weight_spec(shard) for shard in range(shards)],
            out_specs=out_spec,
        ),
        out_shape=jax.ShapeDtypeStruct((tokens, width), jnp.float32),
        compiler_params=params(24),
        cost_estimate=pl.CostEstimate(
            flops=2 * tokens * width * deep * shards,
            bytes_accessed=2 * shards * width * deep,
            transcendentals=0,
        ),
        name="gate_step",
    )(scalars, *([acc] if has_acc else []), *pieces, *([weight] * shards))


def close_kernel(extra, scal, acc, early, late, weight, acts, lam, gconv, gquery, packet, gate):
    step = pl.program_id(0)
    half = early.shape[0]
    tokens = 2 * half
    poles = lam.shape[0]
    groups = weight.shape[0] // LANES
    if groups * pl.num_programs(0) < ROWS:

        @pl.when(step == 0)
        def _():
            gate[...] = jnp.zeros(gate.shape, gate.dtype)

    for part, piece in enumerate((early, late)):
        value = acc[pl.ds(part * half, half), :] + lax.dot_general(
            piece[...], weight[...], NT, preferred_element_type=jnp.float32
        )
        for group in range(groups):
            start = part * half * ROWS + step * groups + group
            gate[pl.ds(start, half, stride=ROWS), :] = value[:, group * LANES:(group + 1) * LANES]

    @pl.when(step == pl.num_programs(0) - 1)
    def _():
        def body(n, state):
            at = tile(tokens - 1 - n)
            grad = gate[at, :]
            conv = grad * acts[0, at, :]
            gconv[at, :] = conv
            gquery[at, :] = grad * acts[3, at, :]
            return tuple(lam[m] * state[m] + conv for m in range(poles))

        zero = jnp.zeros((ROWS, LANES), jnp.float32)
        state = lax.fori_loop(0, tokens, body, (zero,) * poles, unroll=8)
        for m in range(poles):
            packet[m] = state[m]
        for row in range(extra - 1):
            packet[poles + row] = gconv[tile(row), :]
        for row in range(extra):
            packet[poles + extra - 1 + row] = gquery[tile(row), :]


def close_gate(acc, pieces, scalars, weight, acts, lam, extra):
    half, deep = pieces[0].shape
    width = weight.shape[0]
    block = min(256, width)
    tokens = 2 * half
    poles = lam.shape[0]
    flat = (tokens * ROWS, LANES)
    packed = (poles + 2 * extra - 1, ROWS, LANES)
    return pl.pallas_call(
        functools.partial(close_kernel, extra),
        grid_spec=pltpu.PrefetchScalarGridSpec(
            num_scalar_prefetch=1,
            grid=(width // block,),
            in_specs=[
                pl.BlockSpec((tokens, block), lambda i, s: (0, i)),
                whole((half, deep)),
                whole((half, deep)),
                pl.BlockSpec((block, deep), lambda i, s: (i, s[0])),
                whole(acts.shape),
                whole(lam.shape),
            ],
            out_specs=[whole(flat), whole(flat), whole(packed)],
            scratch_shapes=[pltpu.VMEM(flat, jnp.float32)],
        ),
        out_shape=[
            jax.ShapeDtypeStruct(flat, jnp.float32),
            jax.ShapeDtypeStruct(flat, jnp.float32),
            jax.ShapeDtypeStruct(packed, jnp.float32),
        ],
        compiler_params=params(32),
        cost_estimate=pl.CostEstimate(
            flops=2 * tokens * width * deep, bytes_accessed=8 * width * deep, transcendentals=0
        ),
        name="close_gate",
    )(scalars, acc, *pieces, weight, acts, lam)


def scan_kernel(
    taps, scal, gconv, gquery, acts, lam, grow, residues, filters, entering, halo, kv_halo,
    weight, proj, total, first, second, spread, buffer, sem,
):
    extra = taps - 1
    tokens, width = proj.shape[1:]
    poles = lam.shape[0]
    deep = buffer.shape[1]
    copy = pltpu.make_async_copy(
        weight.at[:, pl.ds(pl.multiple_of(scal[0] * deep, deep), deep), :], buffer, sem
    )
    copy.start()

    state = [entering[m] for m in range(poles)]
    keys, values, queries = [], [], []
    for row in range(extra):
        if row:
            state = [(state[m] - halo[row - 1]) * grow[m] for m in range(poles)]
        product = tree_sum([residues[m] * state[m] for m in range(poles)])
        keys.append(product * kv_halo[1, row])
        values.append(product * kv_halo[0, row])
        queries.append(halo[extra - 1 + row])

    def body(n, carry):
        state, sums, later = carry
        at = tile(tokens - 1 - n)
        conv = gconv[at, :]
        key = acts[1, at, :]
        value = acts[2, at, :]
        both = key * value
        state = tuple(lam[m] * state[m] + conv for m in range(poles))
        product = tree_sum([residues[m] * state[m] for m in range(poles)])
        sums = tuple(sums[m] + both * state[m] for m in range(poles))
        now = (gquery[at, :], product * value, product * key)
        for which in range(3):
            spread[which, at, :] = tree_sum(
                [filters[which, 0] * now[which]]
                + [filters[which, lag] * later[which][lag - 1] for lag in range(1, taps)]
            )
        later = tuple((now[which],) + later[which][:-1] for which in range(3))
        return state, sums, later

    zero = jnp.zeros((ROWS, LANES), jnp.float32)
    carry = (
        tuple(entering[m] for m in range(poles)),
        (zero,) * poles,
        (tuple(queries), tuple(keys), tuple(values)),
    )
    _, sums, _ = lax.fori_loop(0, tokens, body, carry, unroll=4)
    for m in range(poles):
        total[m] = sums[m]
    for which in range(3):
        for group in range(width // LANES):
            proj[which, :, pl.ds(group * LANES, LANES)] = spread[
                which, pl.ds(group, tokens, stride=ROWS), :
            ].astype(jnp.bfloat16)
    copy.wait()
    half = deep // 2
    block = min(256, half)
    for part, out in enumerate((first, second)):
        for start in range(0, half, block):
            value = tree_sum([
                lax.dot_general(
                    buffer[which, pl.ds(part * half + start, block), :], proj[which],
                    NT, preferred_element_type=jnp.float32,
                )
                for which in range(3)
            ])
            out[pl.ds(start, block), :] = value.astype(jnp.bfloat16)


def scan_block(chunk, gconv, gquery, acts, lam, grow, residues, filters, entering, halo, kv_halo,
               weight, deep, width):
    tokens = gconv.shape[0] // ROWS
    poles = lam.shape[0]
    taps = filters.shape[1]
    vmem = pl.BlockSpec(memory_space=pltpu.VMEM)
    return pl.pallas_call(
        functools.partial(scan_kernel, taps),
        in_specs=[pl.BlockSpec(memory_space=pltpu.SMEM)] + [vmem] * 10
        + [pl.BlockSpec(memory_space=pl.ANY)],
        out_specs=[vmem] * 4,
        out_shape=[
            jax.ShapeDtypeStruct((3, tokens, width), jnp.bfloat16),
            jax.ShapeDtypeStruct((poles, ROWS, LANES), jnp.float32),
            jax.ShapeDtypeStruct((deep // 2, tokens), jnp.bfloat16),
            jax.ShapeDtypeStruct((deep // 2, tokens), jnp.bfloat16),
        ],
        scratch_shapes=[
            pltpu.VMEM((3, tokens * ROWS, LANES), jnp.float32),
            pltpu.VMEM((3, deep, width), jnp.bfloat16),
            pltpu.SemaphoreType.DMA,
        ],
        compiler_params=params(36),
        cost_estimate=pl.CostEstimate(
            flops=6 * tokens * width * deep, bytes_accessed=16 * width * deep, transcendentals=0
        ),
        name="scan",
    )(chunk, gconv, gquery, acts, lam, grow, residues, filters, entering, halo, kv_halo, weight)


def project_kernel(scal, proj, weight, out):
    out[0] = tree_sum([
        lax.dot_general(weight[which], proj[which], NT, preferred_element_type=jnp.float32)
        for which in range(3)
    ]).astype(out.dtype)


def project(chunks, proj, weight, deep):
    _, tokens, width = proj.shape
    half = deep // 2
    count = 2 * chunks.shape[0]
    return pl.pallas_call(
        project_kernel,
        grid_spec=pltpu.PrefetchScalarGridSpec(
            num_scalar_prefetch=1,
            grid=(count,),
            in_specs=[
                whole(proj.shape),
                pl.BlockSpec((3, half, width), lambda i, s: (0, 2 * s[i // 2] + i % 2, 0)),
            ],
            out_specs=pl.BlockSpec((1, half, tokens), lambda i, s: (i, 0, 0)),
        ),
        out_shape=jax.ShapeDtypeStruct((count, half, tokens), jnp.bfloat16),
        compiler_params=params(24),
        cost_estimate=pl.CostEstimate(
            flops=6 * tokens * width * half * count,
            bytes_accessed=6 * width * half * count,
            transcendentals=0,
        ),
        name="project",
    )(chunks, proj, weight)


def scalars(*values):
    return jnp.stack([jnp.asarray(value, jnp.int32) for value in values])


def tiles(array):
    lead = array.shape[:-1]
    groups = array.shape[-1] // LANES
    array = array.reshape(lead + (groups, LANES))
    if groups < ROWS:
        array = jnp.pad(array, [(0, 0)] * len(lead) + [(0, ROWS - groups), (0, 0)])
    return array


def local(features, saved_conv, grad_out, out_weight, in_weight, short_taps, residues, decay_time):
    f32, bf16 = jnp.float32, jnp.bfloat16
    tokens, width = saved_conv.shape
    taps = short_taps.shape[1]
    extra = taps - 1
    poles = residues.shape[0]
    count = lax.axis_size("chan")
    me = lax.axis_index("chan")
    upper = (me >= count // 2).astype(jnp.int32)
    deep = in_weight.shape[1] // count
    blocks = lax.axis_size("ctx")
    core = lax.axis_index("ctx") % 2

    rate = tiles(1.0 / decay_time)
    lam = jnp.exp(-rate)
    grow = jnp.exp(rate)
    span = jnp.exp(-rate * tokens)
    res = tiles(residues)
    filters = tiles(short_taps)

    half = tokens // 2
    right = left = [grad_out[:half], grad_out[half:]]
    acts = spread_acts(features, saved_conv)
    acc = gate_step(None, right, scalars(me), out_weight, 1, False)
    kv_halo = acts[1:3].reshape(2, tokens, ROWS, LANES)[:, :extra]
    kv_halo = lax.ppermute(kv_halo, "ctx", [(i, i - 1) for i in range(1, blocks)])
    for phase in range(1, count - 1):
        to_right = [(i, i + 1) for i in range(phase - 1, count - 1)]
        to_left = [(i, i - 1) for i in range(1, count - phase + 1)]
        right = [lax.ppermute(piece, "chan", to_right) for piece in right]
        left = [lax.ppermute(piece, "chan", to_left) for piece in left]
        below = jnp.maximum(me - phase, 0)
        above = jnp.minimum(me + phase, count - 1)
        if 2 * phase < count:
            acc = gate_step(acc, right + left, scalars(below, above), out_weight, 2, False)
        else:
            which = jnp.where(upper > 0, below, above)
            acc = gate_step(acc, right + left, scalars(which, upper), out_weight, 1, True)
    last = [
        lax.ppermute(jnp.where(upper > 0, a, b), "chan", [(count - 2, count - 1), (1, 0)])
        for a, b in zip(right, left)
    ]
    which = jnp.where(upper > 0, jnp.maximum(me - count + 1, 0), jnp.minimum(me + count - 1, count - 1))
    gconv, gquery, packet = close_gate(acc, last, scalars(which), out_weight, acts, lam, extra)

    other = lax.ppermute(packet, "ctx", [(i, i ^ 1) for i in range(blocks)])
    first = jnp.where(core == 0, packet, other)
    second = jnp.where(core == 0, other, packet)
    chip = jnp.concatenate([first[:poles] + span * second[:poles], first[poles:]])
    chips = blocks // 2
    arrived = [
        lax.ppermute(
            chip if hop == 1 else chip[:poles], "ctx",
            [(i, i - 2 * hop) for i in range(2 * hop, blocks)],
        )
        for hop in range(1, chips)
    ]
    beyond = sum(
        jnp.exp(-rate * (2 * tokens * (hop - 1))) * arrived[hop - 1][:poles]
        for hop in range(1, chips)
    )
    entering = jnp.where(core == 0, second[:poles] + span * beyond, beyond)
    halo = jnp.where(core == 0, second[poles:], arrived[0][poles:])

    def single(phase):
        return jnp.where(
            upper > 0, jnp.maximum(me - (count - phase), 0), jnp.minimum(me + count - phase, count - 1)
        )

    proj, total, *sent = scan_block(
        scalars(single(1)), gconv, gquery, acts, lam, grow, res, filters, entering, halo, kv_halo,
        in_weight, deep, width,
    )
    order = []
    for phase in range(2, count):
        if 2 * phase <= count:
            order.append(single(phase))
        else:
            order.append(jnp.minimum(me + count - phase, count - 1))
            order.append(jnp.maximum(me - (count - phase), 0))
    order.append(me)
    parts = project(scalars(*order), proj, in_weight, deep)

    come = [lax.ppermute(piece, "chan", [(0, 1), (count - 1, count - 2)]) for piece in sent]
    from_left, from_right = come, [None, None]

    def added(*values):
        return sum(value.astype(f32) for value in values if value is not None).astype(bf16)

    place = 0
    for phase in range(2, count):
        to_right = [(i, i + 1) for i in range(phase)]
        to_left = [(i, i - 1) for i in range(count - phase, count)]
        for piece in range(2):
            if 2 * phase <= count:
                go = back = added(parts[2 * place + piece], from_left[piece], from_right[piece])
            else:
                if from_right[piece] is None:
                    from_right[piece] = from_left[piece]
                go = added(parts[2 * place + piece], from_left[piece])
                back = added(parts[2 * place + 2 + piece], from_right[piece])
            from_left[piece] = lax.ppermute(go, "chan", to_right)
            from_right[piece] = lax.ppermute(back, "chan", to_left)
        place += 1 if 2 * phase <= count else 2
    grad_input = jnp.concatenate(
        [added(parts[2 * place + piece], from_left[piece], from_right[piece]) for piece in range(2)]
    )

    step = 1
    while step < blocks:
        total = total + lax.ppermute(total, "ctx", [(i, i ^ step) for i in range(blocks)])
        step *= 2
    grad_residue = total[:, :width // LANES].reshape(poles, width) / (tokens * blocks)
    return grad_input, grad_residue


def solution(mesh):
    return jax.shard_map(
        local,
        mesh=mesh,
        in_specs=(
            P(None, "ctx", "chan"),
            P("ctx", "chan"),
            P("ctx", "chan"),
            P("chan", None),
            P(None, None, "chan"),
            P(None, None, "chan"),
            P(None, "chan"),
            P(None, "chan"),
        ),
        out_specs=(P("chan", "ctx"), P(None, "chan")),
        check_vma=False,
    )
```

```python
import functools

import jax
import jax.numpy as jnp
from jax import lax
from jax.experimental import pallas as pl
from jax.experimental.pallas import tpu as pltpu
from jax.sharding import PartitionSpec as P

LANES = 128
ROWS = 8
NT = (((1,), (1,)), ((), ()))
VMEM = pl.BlockSpec(memory_space=pltpu.VMEM)
HBM = pl.BlockSpec(memory_space=pltpu.HBM)
SMEM = pl.BlockSpec(memory_space=pltpu.SMEM)
GRANT = 46 * 2**20


def tile(token):
    return pl.ds(pl.multiple_of(token * ROWS, ROWS), ROWS)


def tree_sum(terms):
    terms = list(terms)
    while len(terms) > 1:
        paired = [a + b for a, b in zip(terms[::2], terms[1::2])]
        terms = paired + terms[2 * len(paired):]
    return terms[0]


def spread_kernel(features, saved, *outs):
    tokens, width = saved.shape
    if width < ROWS * LANES:
        for out in outs:
            out[...] = jnp.zeros(out.shape, out.dtype)
    for group in range(width // LANES):
        columns = pl.ds(group * LANES, LANES)
        rows = pl.ds(group, tokens, stride=ROWS)
        for which in range(3):
            outs[which][rows, :] = features[which, :, columns].astype(jnp.float32)
        outs[3][rows, :] = saved[:, columns].astype(jnp.float32)
        outs[4][rows, :] = (
            features[1, :, columns].astype(jnp.float32) * features[2, :, columns].astype(jnp.float32)
        )


def spread_acts(features, saved):
    flat = jax.ShapeDtypeStruct((saved.shape[0] * ROWS, LANES), jnp.float32)
    return pl.pallas_call(
        spread_kernel,
        in_specs=[VMEM] * 2,
        out_specs=[VMEM] * 5,
        out_shape=[flat] * 5,
        compiler_params=pltpu.CompilerParams(vmem_limit_bytes=GRANT),
        name="spread",
    )(features, saved)


def gate_kernel(at, has_acc, shards, count, plan, *refs):
    scal = [plan[at + i] for i in range(2 * shards)]
    acc = refs[0] if has_acc else None
    pieces = [piece[...] for piece in refs[has_acc:has_acc + count]]
    weight, out, buffer, sems = refs[has_acc + count:]
    width, deep = buffer.shape[2:]
    block = min(256, width)
    copies = []
    for shard in range(shards):
        columns = pl.ds(pl.multiple_of(scal[shard] * deep, deep), deep)
        copies.append(
            pltpu.make_async_copy(weight.at[:, columns], buffer.at[shard, 0], sems.at[shard])
        )
        copies[-1].start()
    if shards < count:
        pieces = [jnp.where(scal[1] > 0, *pieces)]
    elif shards > 1:
        pieces = [
            jnp.where(scal[shards + i] > 0, piece, jnp.zeros_like(piece))
            for i, piece in enumerate(pieces)
        ]
    for shard in range(shards):
        copies[shard].wait()
        for start in range(0, width, block):
            rows = pl.ds(start, block)
            value = lax.dot_general(
                pieces[shard], buffer[shard, 0, rows, :], NT, preferred_element_type=jnp.float32
            )
            if shard:
                value = value + out[:, rows]
            elif has_acc:
                value = value + acc[:, rows]
            out[:, rows] = value


def gate_step(plan, at, acc, pieces, weight, shards):
    tokens, deep = pieces[0].shape
    width = weight.shape[0]
    has_acc = acc is not None
    return pl.pallas_call(
        functools.partial(gate_kernel, at, has_acc, shards, len(pieces)),
        in_specs=[SMEM] + [VMEM] * (has_acc + len(pieces))
        + [HBM],
        out_specs=VMEM,
        out_shape=jax.ShapeDtypeStruct((tokens, width), jnp.float32),
        scratch_shapes=[
            pltpu.VMEM((shards, 1, width, deep), jnp.bfloat16),
            pltpu.SemaphoreType.DMA((shards,)),
        ],
        compiler_params=pltpu.CompilerParams(vmem_limit_bytes=GRANT),
        cost_estimate=pl.CostEstimate(
            flops=2 * tokens * width * deep * shards,
            bytes_accessed=2 * shards * width * deep,
            transcendentals=0,
        ),
        name="gate_step",
    )(plan, *([acc] if has_acc else []), *pieces, weight)


def close_kernel(at_plan, extra, plan, acc, piece, weight, query, saved, lam, gconv, gquery, packet, gate):
    tokens, width = acc.shape
    poles = lam.shape[0]
    block = min(256, width)
    if width < ROWS * LANES:
        gate[...] = jnp.zeros(gate.shape, gate.dtype)
    arrived = jnp.where(plan[at_plan] > 0, piece[...], jnp.zeros(piece.shape, piece.dtype))
    for start in range(0, width, block):
        columns = pl.ds(start, block)
        value = acc[:, columns] + lax.dot_general(
            arrived, weight[columns, :], NT, preferred_element_type=jnp.float32
        )
        for group in range(block // LANES):
            rows = pl.ds(start // LANES + group, tokens, stride=ROWS)
            gate[rows, :] = value[:, group * LANES:(group + 1) * LANES]

    def body(n, state):
        at = tile(tokens - 1 - n)
        grad = gate[at, :]
        conv = grad * query[at, :]
        gconv[at, :] = conv
        gquery[at, :] = grad * saved[at, :]
        return tuple(lam[m] * state[m] + conv for m in range(poles))

    zero = jnp.zeros((ROWS, LANES), jnp.float32)
    state = lax.fori_loop(0, tokens, body, (zero,) * poles, unroll=8)
    for m in range(poles):
        packet[m] = state[m]
    for row in range(extra - 1):
        packet[poles + row] = gconv[tile(row), :]
    for row in range(extra):
        packet[poles + extra - 1 + row] = gquery[tile(row), :]


def close_gate(plan, at, acc, piece, weight, query, saved, lam, extra):
    tokens, deep = piece.shape
    width = weight.shape[0]
    poles = lam.shape[0]
    flat = (tokens * ROWS, LANES)
    return pl.pallas_call(
        functools.partial(close_kernel, at, extra),
        in_specs=[SMEM] + [VMEM] * 6,
        out_specs=[VMEM] * 3,
        out_shape=[
            jax.ShapeDtypeStruct(flat, jnp.float32),
            jax.ShapeDtypeStruct(flat, jnp.float32),
            jax.ShapeDtypeStruct((poles + 2 * extra - 1, ROWS, LANES), jnp.float32),
        ],
        scratch_shapes=[pltpu.VMEM(flat, jnp.float32)],
        compiler_params=pltpu.CompilerParams(vmem_limit_bytes=GRANT),
        cost_estimate=pl.CostEstimate(
            flops=2 * tokens * width * deep, bytes_accessed=8 * width * deep, transcendentals=0
        ),
        name="close_gate",
    )(plan, acc, piece, weight, query, saved, lam)


def fold_kernel(plan, own, other, span, chip):
    poles = span.shape[0]
    first = plan[0] % 2 == 0
    for row in range(own.shape[0]):
        value = jnp.where(first, own[row], other[row])
        if row < poles:
            value = value + span[row] * jnp.where(first, other[row], own[row])
        chip[row] = value.astype(chip.dtype)


def fold(plan, own, other, span):
    return pl.pallas_call(
        fold_kernel,
        in_specs=[SMEM] + [VMEM] * 3,
        out_specs=VMEM,
        out_shape=jax.ShapeDtypeStruct(own.shape, jnp.bfloat16),
        compiler_params=pltpu.CompilerParams(vmem_limit_bytes=GRANT),
        name="fold",
    )(plan, own, other, span)


def scan_kernel(
    at_plan, taps, chips, plan, gconv, gquery, key_acts, value_acts, lam, rate, residues, filters, kv_halo,
    own, other, *refs,
):
    arrived = refs[:chips - 1]
    weight, proj, chunk, entering, passed, spread, buffer, sem = refs[chips - 1:]
    extra = taps - 1
    tokens, width = proj.shape[1:]
    poles = lam.shape[0]
    deep = buffer.shape[1]
    copy = pltpu.make_async_copy(
        weight.at[:, pl.ds(pl.multiple_of(plan[at_plan] * deep, deep), deep), :], buffer, sem
    )
    copy.start()

    block = plan[0]
    core, here = block % 2, block // 2
    for m in range(poles):
        beyond = []
        for mask in range(1, chips):
            there = here ^ mask
            distance = (2 * tokens * jnp.maximum(there - here - 1, 0)).astype(jnp.float32)
            term = jnp.exp(-rate[m] * distance) * arrived[mask - 1][m].astype(jnp.float32)
            beyond.append(jnp.where(there > here, term, jnp.zeros_like(term)))
        beyond = tree_sum(beyond)
        entering[m] = jnp.where(
            core == 0, other[m] + jnp.exp(-rate[m] * tokens) * beyond, beyond
        )
    halo = []
    for row in range(poles, poles + 2 * extra - 1):
        value = jnp.where(core == 0, other[row], jnp.zeros_like(other[row]))
        for mask in range(1, chips):
            there = here ^ mask
            value = jnp.where(
                (core == 1) & (there == here + 1), arrived[mask - 1][row].astype(jnp.float32), value
            )
        halo.append(value)

    state = [entering[m] for m in range(poles)]
    keys, values, queries = [], [], []
    for row in range(extra):
        if row:
            state = [(state[m] - halo[row - 1]) * jnp.exp(rate[m]) for m in range(poles)]
        product = tree_sum([residues[m] * state[m] for m in range(poles)])
        keys.append(product * kv_halo[1, row])
        values.append(product * kv_halo[0, row])
        queries.append(halo[extra - 1 + row])

    def body(n, carry):
        state, later = carry
        at = tile(tokens - 1 - n)
        conv = gconv[at, :]
        passed[at, :] = conv
        state = tuple(lam[m] * state[m] + conv for m in range(poles))
        product = tree_sum([residues[m] * state[m] for m in range(poles)])
        now = (gquery[at, :], product * value_acts[at, :], product * key_acts[at, :])
        for which in range(3):
            spread[which, at, :] = tree_sum(
                [filters[which, 0] * now[which]]
                + [filters[which, lag] * later[which][lag - 1] for lag in range(1, taps)]
            )
        return state, tuple((now[which],) + later[which][:-1] for which in range(3))

    carry = (
        tuple(entering[m] for m in range(poles)),
        (tuple(queries), tuple(keys), tuple(values)),
    )
    lax.fori_loop(0, tokens, body, carry, unroll=8)
    for which in range(3):
        for group in range(width // LANES):
            proj[which, :, pl.ds(group * LANES, LANES)] = spread[
                which, pl.ds(group, tokens, stride=ROWS), :
            ].astype(jnp.bfloat16)
    copy.wait()
    project_rows(buffer, proj, chunk)


def project_rows(weight, proj, out):
    rows = out.shape[0]
    block = min(256, rows)
    for start in range(0, rows, block):
        value = tree_sum([
            lax.dot_general(
                weight[which, pl.ds(start, block), :], proj[which],
                NT, preferred_element_type=jnp.float32,
            )
            for which in range(3)
        ])
        out[pl.ds(start, block), :] = value.astype(out.dtype)


def scan_block(plan, at, gconv, gquery, keys, values, lam, rate, residues, filters, kv_halo, own, other,
               arrived, weight, deep, width):
    tokens = gconv.shape[0] // ROWS
    taps = filters.shape[1]
    return pl.pallas_call(
        functools.partial(scan_kernel, at, taps, len(arrived) + 1),
        in_specs=[SMEM] + [VMEM] * (11 + len(arrived))
        + [HBM],
        out_specs=[VMEM] * 4,
        out_shape=[
            jax.ShapeDtypeStruct((3, tokens, width), jnp.bfloat16),
            jax.ShapeDtypeStruct((deep, tokens), jnp.bfloat16),
            jax.ShapeDtypeStruct(lam.shape, jnp.float32),
            jax.ShapeDtypeStruct(gconv.shape, jnp.float32),
        ],
        scratch_shapes=[
            pltpu.VMEM((3, tokens * ROWS, LANES), jnp.float32),
            pltpu.VMEM((3, deep, width), jnp.bfloat16),
            pltpu.SemaphoreType.DMA,
        ],
        compiler_params=pltpu.CompilerParams(vmem_limit_bytes=GRANT),
        cost_estimate=pl.CostEstimate(
            flops=6 * tokens * width * deep, bytes_accessed=16 * width * deep, transcendentals=0
        ),
        name="scan",
    )(plan, gconv, gquery, keys, values, lam, rate, residues, filters, kv_halo, own, other, *arrived,
      weight)


def total_kernel(gconv, product, lam, entering, total):
    tokens = gconv.shape[0] // ROWS
    poles = lam.shape[0]

    def body(n, carry):
        state, sums = carry
        at = tile(tokens - 1 - n)
        conv, both = gconv[at, :], product[at, :]
        state = tuple(lam[m] * state[m] + conv for m in range(poles))
        return state, tuple(sums[m] + both * state[m] for m in range(poles))

    state = tuple(entering[m] for m in range(poles))
    zero = jnp.zeros((ROWS, LANES), jnp.float32)
    _, sums = lax.fori_loop(0, tokens, body, (state, (zero,) * poles), unroll=8)
    for m in range(poles):
        total[m] = sums[m]


def residue_total(gconv, product, lam, entering):
    return pl.pallas_call(
        total_kernel,
        in_specs=[VMEM] * 4,
        out_specs=VMEM,
        out_shape=jax.ShapeDtypeStruct(lam.shape, jnp.float32),
        compiler_params=pltpu.CompilerParams(vmem_limit_bytes=GRANT),
        cost_estimate=pl.CostEstimate(
            flops=4 * gconv.size * lam.shape[0], bytes_accessed=8 * gconv.size, transcendentals=0
        ),
        name="residue_total",
    )(gconv, product, lam, entering)


def project_kernel(at, count, plan, proj, weight, *refs):
    outs, buffer, sems = refs[:count], refs[count], refs[count + 1]
    deep = buffer.shape[2]
    copies = [
        pltpu.make_async_copy(
            weight.at[:, pl.ds(pl.multiple_of(plan[at + i] * deep, deep), deep), :],
            buffer.at[i], sems.at[i],
        )
        for i in range(count)
    ]
    for copy in copies:
        copy.start()
    for i in range(count):
        copies[i].wait()
        project_rows(buffer.at[i], proj, outs[i])


def project(plan, at, count, proj, weight, deep):
    _, tokens, width = proj.shape
    return pl.pallas_call(
        functools.partial(project_kernel, at, count),
        in_specs=[SMEM, VMEM, HBM],
        out_specs=[VMEM] * count,
        out_shape=[jax.ShapeDtypeStruct((deep, tokens), jnp.bfloat16)] * count,
        scratch_shapes=[
            pltpu.VMEM((count, 3, deep, width), jnp.bfloat16),
            pltpu.SemaphoreType.DMA((count,)),
        ],
        compiler_params=pltpu.CompilerParams(vmem_limit_bytes=GRANT),
        cost_estimate=pl.CostEstimate(
            flops=6 * tokens * width * deep * count,
            bytes_accessed=6 * width * deep * count,
            transcendentals=0,
        ),
        name="project",
    )(plan, proj, weight)


def scalars(*values):
    return jnp.stack([jnp.asarray(value, jnp.int32) for value in values])


def tiles(array):
    lead = array.shape[:-1]
    groups = array.shape[-1] // LANES
    array = array.reshape(lead + (groups, LANES))
    if groups < ROWS:
        array = jnp.pad(array, [(0, 0)] * len(lead) + [(0, ROWS - groups), (0, 0)])
    return array


def swap_even(value, count):
    return lax.ppermute(value, "chan", [(i, i ^ 1) for i in range(count)])


def swap_odd(value, count, blocks):
    pairs = []
    for block in range(blocks):
        for i in range(count):
            other = i + 1 if i % 2 else i - 1
            if 0 <= other < count:
                pairs.append((block * count + i, block * count + other))
            else:
                pairs.append((block * count + i, (block ^ 1) * count + i))
    return lax.ppermute(value, ("ctx", "chan"), pairs)


def swap_ctx(value, mask, blocks):
    return lax.ppermute(value, "ctx", [(i, i ^ mask) for i in range(blocks)])


def tie(*values):
    return lax.optimization_barrier(values)


def local(features, saved_conv, grad_out, out_weight, in_weight, short_taps, residues, decay_time):
    f32, bf16 = jnp.float32, jnp.bfloat16
    tokens, width = saved_conv.shape
    taps = short_taps.shape[1]
    extra = taps - 1
    poles = residues.shape[0]
    count = lax.axis_size("chan")
    me = lax.axis_index("chan")
    even = me % 2 == 0
    deep = in_weight.shape[1] // count
    blocks = lax.axis_size("ctx")
    block = lax.axis_index("ctx")

    rate = tiles(1.0 / decay_time)
    lam = jnp.exp(-rate)
    span = jnp.exp(-rate * tokens)
    res = tiles(residues)
    filters = tiles(short_taps)

    def shared(phase):
        far = count - phase
        as_even = jnp.where(me < phase, me + far, jnp.maximum(me - far + 1, 0))
        as_odd = jnp.where(me >= far, me - far, jnp.minimum(me + far - 1, count - 1))
        return jnp.where(even, as_even, as_odd)

    def reached(phase, along):
        right = jnp.minimum(me + count - phase, count - 1)
        left = jnp.maximum(me - (count - phase), 0)
        return jnp.where(along, right, left)

    def shards(phase):
        above, below = me + phase, me - phase
        high, low = jnp.minimum(above, count - 1), jnp.maximum(below, 0)
        at_even, at_odd = jnp.where(even, high, low), jnp.where(even, low, high)
        even_ok = jnp.where(even, above < count, below >= 0)
        odd_ok = jnp.where(even, below >= 0, above < count)
        if 2 * phase == count:
            return [jnp.where(even_ok, at_even, at_odd), even_ok]
        return [at_even, at_odd, even_ok, odd_ok]

    edge = (me == 0) | (me == count - 1)
    plan, places = [block, edge], {}

    def planned(name, values):
        places[name] = len(plan)
        plan.extend(values)

    planned("own", [me, 1])
    for phase in range(1, count - 1):
        planned(("gate", phase), shards(phase))
    planned("first", [shared(1)])
    chunks = []
    for phase in range(2, count):
        if 2 * phase <= count:
            chunks.append(shared(phase))
        else:
            chunks.append(reached(phase, even))
            if phase + 1 < count:
                chunks.append(reached(phase + 1, ~even))
    chunks.append(me)
    planned("chunks", chunks)
    plan = scalars(*plan)

    evens = swap_even(grad_out, count)
    odds = swap_odd(grad_out, count, blocks)
    query, keys, values, saved, product = spread_acts(features, saved_conv)
    acc = gate_step(plan, places["own"], None, [grad_out], out_weight, 1)
    kv_halo = tiles(features[1:3, :extra].astype(f32))
    kv_halo = lax.ppermute(kv_halo, "ctx", [(i, (i - 1) % blocks) for i in range(blocks)])
    last = jnp.where(even, jnp.minimum(count - 1, me + count - 1), jnp.maximum(me - count + 1, 0))
    last_weight = lax.dynamic_slice(out_weight, (0, last * width), (width, width))
    (
        evens, odds, acc, plan, query, keys, values, saved, product, rate, lam, span, res, filters
    ) = tie(evens, odds, acc, plan, query, keys, values, saved, product, rate, lam, span, res, filters)
    for phase in range(1, count - 1):
        next_evens = swap_even(odds, count)
        next_odds = swap_odd(evens, count, blocks)
        acc = gate_step(
            plan, places["gate", phase], acc, [evens, odds], out_weight,
            1 if 2 * phase == count else 2,
        )
        evens, odds = next_evens, next_odds
        if phase == 1:
            evens, odds, acc, kv_halo, last_weight = tie(evens, odds, acc, kv_halo, last_weight)
        elif phase < count - 2:
            evens, odds, acc = tie(evens, odds, acc)
    gconv, gquery, packet = close_gate(plan, 1, acc, evens, last_weight, query, saved, lam, extra)

    other = swap_ctx(packet, 1, blocks)
    chip = fold(plan, packet, other, span)
    arrived = [swap_ctx(chip, 2 * mask, blocks) for mask in range(1, blocks // 2)]

    def added(*parts):
        return sum(value.astype(f32) for value in parts if value is not None).astype(bf16)

    proj, part, entering, gconv = scan_block(
        plan, places["first"], gconv, gquery, keys, values, lam, rate, res, filters, kv_halo,
        packet, other, arrived, in_weight, deep, width,
    )
    for_even, for_odd = {1: part}, {2: part}
    parts = list(project(plan, places["chunks"], len(chunks), proj, in_weight, deep))
    evens, odds = swap_even(part, count), None
    evens, gconv, *parts = tie(evens, gconv, *parts)
    for phase in range(2, count):
        for_even[phase] = parts.pop(0)
        if 2 * phase <= count:
            for_odd[phase + 1] = for_even[phase]
        elif phase + 1 < count:
            for_odd[phase + 1] = parts.pop(0)
    total = residue_total(gconv, product, lam, entering)
    for phase in range(2, count):
        if odds is not None:
            odds = jnp.where(edge, jnp.zeros_like(odds), odds)
        next_evens = swap_even(added(for_even[phase], odds), count)
        odds = swap_odd(added(for_odd[phase], evens), count, blocks)
        evens = next_evens
    odds = jnp.where(edge, jnp.zeros_like(odds), odds)
    grad_input = added(parts.pop(0), evens, odds)

    mask = 1
    while mask < blocks:
        total = total + swap_ctx(total, mask, blocks)
        mask *= 2
    grad_residue = total[:, :width // LANES].reshape(poles, width) / (tokens * blocks)
    return grad_input, grad_residue


def solution(mesh):
    return jax.shard_map(
        local,
        mesh=mesh,
        in_specs=(
            P(None, "ctx", "chan"),
            P("ctx", "chan"),
            P("ctx", "chan"),
            P("chan", None),
            P(None, None, "chan"),
            P(None, None, "chan"),
            P(None, "chan"),
            P(None, "chan"),
        ),
        out_specs=(P("chan", "ctx"), P(None, "chan")),
        check_vma=False,
    )
```

```python
import functools

import jax
import jax.numpy as jnp
from jax import lax
from jax.experimental import pallas as pl
from jax.experimental.pallas import tpu as pltpu
from jax.sharding import PartitionSpec as P

LANES = 128
ROWS = 8
NT = (((1,), (1,)), ((), ()))
VMEM = pl.BlockSpec(memory_space=pltpu.VMEM)
HBM = pl.BlockSpec(memory_space=pltpu.HBM)
SMEM = pl.BlockSpec(memory_space=pltpu.SMEM)
GRANT = 46 * 2**20
SMALL = pl.CostEstimate(flops=1, bytes_accessed=1, transcendentals=0)


def tile(token):
    return pl.ds(pl.multiple_of(token * ROWS, ROWS), ROWS)


def tree_sum(terms):
    terms = list(terms)
    while len(terms) > 1:
        paired = [a + b for a, b in zip(terms[::2], terms[1::2])]
        terms = paired + terms[2 * len(paired):]
    return terms[0]


def spread_kernel(features, saved, *outs):
    tokens, width = saved.shape
    if width < ROWS * LANES:
        for out in outs:
            out[...] = jnp.zeros(out.shape, out.dtype)
    for group in range(width // LANES):
        columns = pl.ds(group * LANES, LANES)
        rows = pl.ds(group, tokens, stride=ROWS)
        for which in range(3):
            outs[which][rows, :] = features[which, :, columns].astype(jnp.float32)
        outs[3][rows, :] = saved[:, columns].astype(jnp.float32)
        outs[4][rows, :] = (
            features[1, :, columns].astype(jnp.float32) * features[2, :, columns].astype(jnp.float32)
        )


def spread_acts(features, saved):
    flat = jax.ShapeDtypeStruct((saved.shape[0] * ROWS, LANES), jnp.float32)
    return pl.pallas_call(
        spread_kernel,
        in_specs=[VMEM] * 2,
        out_specs=[VMEM] * 5,
        out_shape=[flat] * 5,
        compiler_params=pltpu.CompilerParams(vmem_limit_bytes=GRANT),
        cost_estimate=SMALL,
        name="spread",
    )(features, saved)


def gate_kernel(at, has_acc, shards, count, halves, plan, *refs):
    acc = refs[0] if has_acc else None
    pieces = [
        jnp.concatenate([refs[has_acc + halves * i + part][...] for part in range(halves)])
        for i in range(count)
    ]
    weight, out, buffer, sems = refs[has_acc + halves * count:]
    width, deep = buffer.shape[1:]
    block = min(256, width)
    copies = []
    for shard in range(shards):
        columns = pl.ds(pl.multiple_of(plan[at + shard] * deep, deep), deep)
        copies.append(
            pltpu.make_async_copy(weight.at[:, columns], buffer.at[shard], sems.at[shard])
        )
        copies[-1].start()
    if shards < count:
        pieces = [jnp.where(plan[at + 1] > 0, *pieces)]
    elif shards > 1:
        pieces = [
            jnp.where(plan[at + shards + i] > 0, piece, jnp.zeros_like(piece))
            for i, piece in enumerate(pieces)
        ]
    for shard in range(shards):
        copies[shard].wait()
        for start in range(0, width, block):
            rows = pl.ds(start, block)
            value = lax.dot_general(
                pieces[shard], buffer[shard, rows, :], NT, preferred_element_type=jnp.float32
            )
            if shard:
                value = value + out[:, rows]
            elif has_acc:
                value = value + acc[:, rows]
            out[:, rows] = value


def gate_step(plan, at, acc, pieces, weight, shards):
    halves = len(pieces[0])
    tokens, deep = halves * pieces[0][0].shape[0], pieces[0][0].shape[1]
    width = weight.shape[0]
    has_acc = acc is not None
    flat = [piece for shard in pieces for piece in shard]
    return pl.pallas_call(
        functools.partial(gate_kernel, at, has_acc, shards, len(pieces), halves),
        in_specs=[SMEM] + [VMEM] * (has_acc + len(flat)) + [HBM],
        out_specs=VMEM,
        out_shape=jax.ShapeDtypeStruct((tokens, width), jnp.float32),
        scratch_shapes=[
            pltpu.VMEM((shards, width, deep), jnp.bfloat16),
            pltpu.SemaphoreType.DMA((shards,)),
        ],
        compiler_params=pltpu.CompilerParams(vmem_limit_bytes=GRANT),
        cost_estimate=SMALL,
        name="gate_step",
    )(plan, *([acc] if has_acc else []), *flat, weight)


def close_kernel(at, extra, late, plan, acc, piece, weight, query, saved, lam, *refs):
    if late:
        gconv, gquery, packet, gate = refs
    else:
        later, gconv, gquery, packet, gate = refs
    tokens = piece.shape[0]
    first = tokens if late else 0
    width = weight.shape[0]
    poles = lam.shape[0]
    block = min(256, width)
    if width < ROWS * LANES:
        gate[...] = jnp.zeros(gate.shape, gate.dtype)
    arrived = jnp.where(plan[at] > 0, piece[...], jnp.zeros(piece.shape, piece.dtype))
    for start in range(0, width, block):
        columns = pl.ds(start, block)
        value = acc[pl.ds(first, tokens), columns] + lax.dot_general(
            arrived, weight[columns, :], NT, preferred_element_type=jnp.float32
        )
        for group in range(block // LANES):
            rows = pl.ds(start // LANES + group, tokens, stride=ROWS)
            gate[rows, :] = value[:, group * LANES:(group + 1) * LANES]

    def body(n, state):
        token = tokens - 1 - n
        here = tile(token)
        there = tile(first + token)
        grad = gate[here, :]
        conv = grad * query[there, :]
        gconv[here, :] = conv
        gquery[here, :] = grad * saved[there, :]
        return tuple(lam[m] * state[m] + conv for m in range(poles))

    if late:
        state = (jnp.zeros((ROWS, LANES), jnp.float32),) * poles
    else:
        state = tuple(later[m] for m in range(poles))
    state = lax.fori_loop(0, tokens, body, state, unroll=8)
    for m in range(poles):
        packet[m] = state[m]
    if not late:
        for row in range(extra - 1):
            packet[poles + row] = gconv[tile(row), :]
        for row in range(extra):
            packet[poles + extra - 1 + row] = gquery[tile(row), :]


def close_gate(plan, at, acc, piece, weight, query, saved, lam, extra, later=None):
    tokens, deep = piece.shape
    width = weight.shape[0]
    poles = lam.shape[0]
    late = later is None
    flat = (tokens * ROWS, LANES)
    packed = (poles if late else poles + 2 * extra - 1, ROWS, LANES)
    return pl.pallas_call(
        functools.partial(close_kernel, at, extra, late),
        in_specs=[SMEM] + [VMEM] * (6 if late else 7),
        out_specs=[VMEM] * 3,
        out_shape=[
            jax.ShapeDtypeStruct(flat, jnp.float32),
            jax.ShapeDtypeStruct(flat, jnp.float32),
            jax.ShapeDtypeStruct(packed, jnp.float32),
        ],
        scratch_shapes=[pltpu.VMEM(flat, jnp.float32)],
        compiler_params=pltpu.CompilerParams(vmem_limit_bytes=GRANT),
        cost_estimate=SMALL,
        name="close_gate",
    )(plan, acc, piece, weight, query, saved, lam, *([] if late else [later]))


def fold_kernel(plan, own, other, span, chip):
    poles = span.shape[0]
    first = plan[0] % 2 == 0
    for row in range(own.shape[0]):
        value = jnp.where(first, own[row], other[row])
        if row < poles:
            value = value + span[row] * jnp.where(first, other[row], own[row])
        chip[row] = value.astype(chip.dtype)


def fold(plan, own, other, span):
    return pl.pallas_call(
        fold_kernel,
        in_specs=[SMEM] + [VMEM] * 3,
        out_specs=VMEM,
        out_shape=jax.ShapeDtypeStruct(own.shape, jnp.bfloat16),
        compiler_params=pltpu.CompilerParams(vmem_limit_bytes=GRANT),
        cost_estimate=SMALL,
        name="fold",
    )(plan, own, other, span)


def scan_kernel(
    at_plan, taps, chips, plan, late_conv, late_query, early_conv, early_query, key_acts, value_acts,
    lam, rate, residues, filters, kv_halo, own, other, *refs,
):
    arrived = refs[:chips - 1]
    weight, proj, chunk, chunk_rest, entering, passed, spread, buffer, sem = refs[chips - 1:]
    extra = taps - 1
    tokens, width = proj.shape[1:]
    poles = lam.shape[0]
    deep = buffer.shape[1]
    copy = pltpu.make_async_copy(
        weight.at[:, pl.ds(pl.multiple_of(plan[at_plan] * deep, deep), deep), :], buffer, sem
    )
    copy.start()

    block = plan[0]
    core, here = block % 2, block // 2
    for m in range(poles):
        beyond = []
        for mask in range(1, chips):
            there = here ^ mask
            distance = (2 * tokens * jnp.maximum(there - here - 1, 0)).astype(jnp.float32)
            term = jnp.exp(-rate[m] * distance) * arrived[mask - 1][m].astype(jnp.float32)
            beyond.append(jnp.where(there > here, term, jnp.zeros_like(term)))
        beyond = tree_sum(beyond)
        entering[m] = jnp.where(
            core == 0, other[m] + jnp.exp(-rate[m] * tokens) * beyond, beyond
        )
    halo = []
    for row in range(poles, poles + 2 * extra - 1):
        value = jnp.where(core == 0, other[row], jnp.zeros_like(other[row]))
        for mask in range(1, chips):
            there = here ^ mask
            value = jnp.where(
                (core == 1) & (there == here + 1), arrived[mask - 1][row].astype(jnp.float32), value
            )
        halo.append(value)

    state = [entering[m] for m in range(poles)]
    keys, values, queries = [], [], []
    for row in range(extra):
        if row:
            state = [(state[m] - halo[row - 1]) * jnp.exp(rate[m]) for m in range(poles)]
        product = tree_sum([residues[m] * state[m] for m in range(poles)])
        keys.append(product * kv_halo[1, row])
        values.append(product * kv_halo[0, row])
        queries.append(halo[extra - 1 + row])

    half = tokens // 2

    def body(first, gconv, gquery, n, carry):
        state, later = carry
        here = tile(half - 1 - n)
        at = tile(first + half - 1 - n)
        conv = gconv[here, :]
        passed[at, :] = conv
        state = tuple(lam[m] * state[m] + conv for m in range(poles))
        product = tree_sum([residues[m] * state[m] for m in range(poles)])
        now = (gquery[here, :], product * value_acts[at, :], product * key_acts[at, :])
        for which in range(3):
            spread[which, at, :] = tree_sum(
                [filters[which, 0] * now[which]]
                + [filters[which, lag] * later[which][lag - 1] for lag in range(1, taps)]
            )
        return state, tuple((now[which],) + later[which][:-1] for which in range(3))

    carry = (
        tuple(entering[m] for m in range(poles)),
        (tuple(queries), tuple(keys), tuple(values)),
    )
    for first, gconv, gquery in ((half, late_conv, late_query), (0, early_conv, early_query)):
        carry = lax.fori_loop(
            0, half, functools.partial(body, first, gconv, gquery), carry, unroll=8
        )
    for which in range(3):
        for group in range(width // LANES):
            proj[which, :, pl.ds(group * LANES, LANES)] = spread[
                which, pl.ds(group, tokens, stride=ROWS), :
            ].astype(jnp.bfloat16)
    copy.wait()
    project_rows(buffer, proj, (chunk, chunk_rest))


def project_rows(weight, proj, outs):
    rows = outs[0].shape[0]
    block = min(256, rows)
    for part, out in enumerate(outs):
        for start in range(0, rows, block):
            value = tree_sum([
                lax.dot_general(
                    weight[which, pl.ds(part * rows + start, block), :], proj[which],
                    NT, preferred_element_type=jnp.float32,
                )
                for which in range(3)
            ])
            out[pl.ds(start, block), :] = value.astype(out.dtype)


def scan_block(plan, at, gated, keys, values, lam, rate, residues, filters, kv_halo, own, other,
               arrived, weight, deep, width):
    tokens = keys.shape[0] // ROWS
    taps = filters.shape[1]
    return pl.pallas_call(
        functools.partial(scan_kernel, at, taps, len(arrived) + 1),
        in_specs=[SMEM] + [VMEM] * (13 + len(arrived))
        + [HBM],
        out_specs=[VMEM] * 5,
        out_shape=[
            jax.ShapeDtypeStruct((3, tokens, width), jnp.bfloat16),
            jax.ShapeDtypeStruct((deep // 2, tokens), jnp.bfloat16),
            jax.ShapeDtypeStruct((deep // 2, tokens), jnp.bfloat16),
            jax.ShapeDtypeStruct(lam.shape, jnp.float32),
            jax.ShapeDtypeStruct(keys.shape, jnp.float32),
        ],
        scratch_shapes=[
            pltpu.VMEM((3, tokens * ROWS, LANES), jnp.float32),
            pltpu.VMEM((3, deep, width), jnp.bfloat16),
            pltpu.SemaphoreType.DMA,
        ],
        compiler_params=pltpu.CompilerParams(vmem_limit_bytes=GRANT),
        cost_estimate=SMALL,
        name="scan",
    )(plan, *gated, keys, values, lam, rate, residues, filters, kv_halo, own, other, *arrived, weight)


def add_up_residues(gconv, product, lam, entering, total):
    tokens = gconv.shape[0] // ROWS
    poles = lam.shape[0]

    def body(n, carry):
        state, sums = carry
        at = tile(tokens - 1 - n)
        conv, both = gconv[at, :], product[at, :]
        state = tuple(lam[m] * state[m] + conv for m in range(poles))
        return state, tuple(sums[m] + both * state[m] for m in range(poles))

    state = tuple(entering[m] for m in range(poles))
    zero = jnp.zeros((ROWS, LANES), jnp.float32)
    _, sums = lax.fori_loop(0, tokens, body, (state, (zero,) * poles), unroll=8)
    for m in range(poles):
        total[m] = sums[m]


def project_kernel(at, count, with_total, plan, proj, weight, *refs):
    if with_total:
        sources, refs = refs[:4], refs[4:]
    outs, refs = refs[:2 * count], refs[2 * count:]
    if with_total:
        total, refs = refs[0], refs[1:]
    buffer, sems = refs
    deep = buffer.shape[2]
    copies = [
        pltpu.make_async_copy(
            weight.at[:, pl.ds(pl.multiple_of(plan[at + i] * deep, deep), deep), :],
            buffer.at[i], sems.at[i],
        )
        for i in range(count)
    ]
    for copy in copies:
        copy.start()
    if with_total:
        add_up_residues(*sources, total)
    for i in range(count):
        copies[i].wait()
        project_rows(buffer.at[i], proj, outs[2 * i:2 * i + 2])


def project(plan, at, count, proj, weight, deep, sources=()):
    _, tokens, width = proj.shape
    outs = [jax.ShapeDtypeStruct((deep // 2, tokens), jnp.bfloat16)] * (2 * count)
    if sources:
        outs.append(jax.ShapeDtypeStruct(sources[-1].shape, jnp.float32))
    return pl.pallas_call(
        functools.partial(project_kernel, at, count, bool(sources)),
        in_specs=[SMEM, VMEM, HBM] + [VMEM] * len(sources),
        out_specs=[VMEM] * len(outs),
        out_shape=outs,
        scratch_shapes=[
            pltpu.VMEM((count, 3, deep, width), jnp.bfloat16),
            pltpu.SemaphoreType.DMA((count,)),
        ],
        compiler_params=pltpu.CompilerParams(vmem_limit_bytes=GRANT),
        cost_estimate=pl.CostEstimate(
            flops=6 * tokens * width * deep * count,
            bytes_accessed=6 * width * deep * count,
            transcendentals=0,
        ),
        name="project",
    )(plan, proj, weight, *sources)


def scalars(*values):
    return jnp.stack([jnp.asarray(value, jnp.int32) for value in values])


def tiles(array):
    lead = array.shape[:-1]
    groups = array.shape[-1] // LANES
    array = array.reshape(lead + (groups, LANES))
    if groups < ROWS:
        array = jnp.pad(array, [(0, 0)] * len(lead) + [(0, ROWS - groups), (0, 0)])
    return array


def swap_even(value, count):
    return lax.ppermute(value, "chan", [(i, i ^ 1) for i in range(count)])


def swap_odd(value, count, blocks):
    pairs = []
    for block in range(blocks):
        for i in range(count):
            other = i + 1 if i % 2 else i - 1
            if 0 <= other < count:
                pairs.append((block * count + i, block * count + other))
            else:
                pairs.append((block * count + i, (block ^ 1) * count + i))
    return lax.ppermute(value, ("ctx", "chan"), pairs)


def swap_ctx(value, mask, blocks):
    return lax.ppermute(value, "ctx", [(i, i ^ mask) for i in range(blocks)])


def tie(*values):
    return lax.optimization_barrier(values)


def local(features, saved_conv, grad_out, out_weight, in_weight, short_taps, residues, decay_time):
    f32, bf16 = jnp.float32, jnp.bfloat16
    tokens, width = saved_conv.shape
    taps = short_taps.shape[1]
    extra = taps - 1
    poles = residues.shape[0]
    count = lax.axis_size("chan")
    me = lax.axis_index("chan")
    even = me % 2 == 0
    deep = in_weight.shape[1] // count
    blocks = lax.axis_size("ctx")
    block = lax.axis_index("ctx")

    rate = tiles(1.0 / decay_time)
    lam = jnp.exp(-rate)
    span = jnp.exp(-rate * tokens)
    res = tiles(residues)
    filters = tiles(short_taps)

    def shared(phase):
        far = count - phase
        as_even = jnp.where(me < phase, me + far, jnp.maximum(me - far + 1, 0))
        as_odd = jnp.where(me >= far, me - far, jnp.minimum(me + far - 1, count - 1))
        return jnp.where(even, as_even, as_odd)

    def reached(phase, along):
        right = jnp.minimum(me + count - phase, count - 1)
        left = jnp.maximum(me - (count - phase), 0)
        return jnp.where(along, right, left)

    def shards(phase):
        above, below = me + phase, me - phase
        high, low = jnp.minimum(above, count - 1), jnp.maximum(below, 0)
        at_even, at_odd = jnp.where(even, high, low), jnp.where(even, low, high)
        even_ok = jnp.where(even, above < count, below >= 0)
        odd_ok = jnp.where(even, below >= 0, above < count)
        if 2 * phase == count:
            return [jnp.where(even_ok, at_even, at_odd), even_ok]
        return [at_even, at_odd, even_ok, odd_ok]

    edge = (me == 0) | (me == count - 1)
    plan, places = [block, edge], {}

    def planned(name, values):
        places[name] = len(plan)
        plan.extend(values)

    planned("own", [me, 1])
    for phase in range(1, count - 1):
        planned(("gate", phase), shards(phase))
    planned("first", [shared(1)])
    chunks = []
    for phase in range(2, count):
        if 2 * phase <= count:
            chunks.append(shared(phase))
        else:
            chunks.append(reached(phase, even))
            if phase + 1 < count:
                chunks.append(reached(phase + 1, ~even))
    chunks.append(me)
    planned("chunks", chunks)
    plan = scalars(*plan)

    half = tokens // 2
    evens = [swap_even(grad_out[half:], count)]
    odds = [swap_odd(grad_out[half:], count, blocks)]
    rest, plan, rate, lam, span, res, filters = tie(grad_out, plan, rate, lam, span, res, filters)
    evens.append(swap_even(rest[:half], count))
    odds.append(swap_odd(rest[:half], count, blocks))
    evens[0], odds[0] = tie(evens[0], odds[0])
    acc = None
    for phase in range(1, count - 1):
        ahead = [[swap_even(odds[0], count)], [swap_odd(evens[0], count, blocks)]]
        if phase == 1:
            acc = gate_step(plan, places["own"], None, [[grad_out]], out_weight, 1)
            evens[1], odds[1], acc = tie(evens[1], odds[1], acc)
        ahead[0].append(swap_even(odds[1], count))
        ahead[1].append(swap_odd(evens[1], count, blocks))
        acc = gate_step(
            plan, places["gate", phase], acc, [evens[::-1], odds[::-1]], out_weight,
            1 if 2 * phase == count else 2,
        )
        evens, odds = ahead
        if phase < count - 2:
            evens[0], odds[0], acc = tie(evens[0], odds[0], acc)
            evens[1], odds[1] = tie(evens[1], odds[1])
        if phase == 1:
            odds[0], features, saved_conv = tie(odds[0], features, saved_conv)
            kv_halo = tiles(features[1:3, :extra].astype(f32))
            kv_halo = lax.ppermute(kv_halo, "ctx", [(i, (i - 1) % blocks) for i in range(blocks)])
            last = jnp.where(
                even, jnp.minimum(count - 1, me + count - 1), jnp.maximum(me - count + 1, 0)
            )
            last_weight = lax.dynamic_slice(out_weight, (0, last * width), (width, width))
            query, keys, values, saved, product = spread_acts(features, saved_conv)
            odds[1], kv_halo, last_weight, query, keys, values, saved, product = tie(
                odds[1], kv_halo, last_weight, query, keys, values, saved, product
            )
    late_conv, late_query, later = close_gate(
        plan, 1, acc, evens[0], last_weight, query, saved, lam, extra
    )
    early_conv, early_query, packet = close_gate(
        plan, 1, acc, evens[1], last_weight, query, saved, lam, extra, later
    )

    other = swap_ctx(packet, 1, blocks)
    chip = fold(plan, packet, other, span)
    arrived = [swap_ctx(chip, 2 * mask, blocks) for mask in range(1, blocks // 2)]

    def added(*parts):
        return sum(value.astype(f32) for value in parts if value is not None).astype(bf16)

    def masked(value):
        return None if value is None else jnp.where(edge, jnp.zeros_like(value), value)

    proj, *part, entering, gconv = scan_block(
        plan, places["first"], [late_conv, late_query, early_conv, early_query], keys, values, lam,
        rate, res, filters, kv_halo, packet, other, arrived, in_weight, deep, width,
    )
    for_even, for_odd = {1: part}, {2: part}
    evens, odds = [swap_even(piece, count) for piece in part], [None, None]
    *parts, total = project(
        plan, places["chunks"], 1, proj, in_weight, deep, [gconv, product, lam, entering]
    )
    evens[0], proj, total, *parts = tie(
        evens[0], proj, total, *parts
    )
    parts += project(plan, places["chunks"] + 1, len(chunks) - 1, proj, in_weight, deep)
    for phase in range(2, count):
        for_even[phase], parts = parts[:2], parts[2:]
        if 2 * phase <= count:
            for_odd[phase + 1] = for_even[phase]
        elif phase + 1 < count:
            for_odd[phase + 1], parts = parts[:2], parts[2:]
    for phase in range(2, count):
        if phase > 2:
            for piece in range(2):
                evens[piece], odds[piece] = tie(evens[piece], odds[piece])
        if phase == count - 1:
            odds[0], total = tie(odds[0], total)
        for piece in range(2):
            next_even = swap_even(added(for_even[phase][piece], masked(odds[piece])), count)
            odds[piece] = swap_odd(added(for_odd[phase][piece], evens[piece]), count, blocks)
            evens[piece] = next_even
    grad_input = jnp.concatenate(
        [added(parts[piece], evens[piece], masked(odds[piece])) for piece in range(2)]
    )

    mask = 1
    while mask < blocks:
        total = total + swap_ctx(total, mask, blocks)
        mask *= 2
    grad_residue = total[:, :width // LANES].reshape(poles, width) / (tokens * blocks)
    return grad_input, grad_residue


def solution(mesh):
    return jax.shard_map(
        local,
        mesh=mesh,
        in_specs=(
            P(None, "ctx", "chan"),
            P("ctx", "chan"),
            P("ctx", "chan"),
            P("chan", None),
            P(None, None, "chan"),
            P(None, None, "chan"),
            P(None, "chan"),
            P(None, "chan"),
        ),
        out_specs=(P("chan", "ctx"), P(None, "chan")),
        check_vma=False,
    )
```

```python
import functools

import jax
import jax.numpy as jnp
from jax import lax
from jax.experimental import pallas as pl
from jax.experimental.pallas import tpu as pltpu
from jax.sharding import PartitionSpec as P

LANES = 128
ROWS = 8
NT = (((1,), (1,)), ((), ()))
VMEM = pl.BlockSpec(memory_space=pltpu.VMEM)
HBM = pl.BlockSpec(memory_space=pltpu.HBM)
SMEM = pl.BlockSpec(memory_space=pltpu.SMEM)
GRANT = 46 * 2**20
TAIL = 16
SMALL = pl.CostEstimate(flops=1, bytes_accessed=1, transcendentals=0)


def tile(token):
    return pl.ds(pl.multiple_of(token * ROWS, ROWS), ROWS)


def tree_sum(terms):
    terms = list(terms)
    while len(terms) > 1:
        paired = [a + b for a, b in zip(terms[::2], terms[1::2])]
        terms = paired + terms[2 * len(paired):]
    return terms[0]


def spread_kernel(features, saved, *outs):
    tokens, width = saved.shape
    if width < ROWS * LANES:
        for out in outs:
            out[...] = jnp.zeros(out.shape, out.dtype)
    for group in range(width // LANES):
        columns = pl.ds(group * LANES, LANES)
        rows = pl.ds(group, tokens, stride=ROWS)
        for which in range(3):
            outs[which][rows, :] = features[which, :, columns].astype(jnp.float32)
        outs[3][rows, :] = saved[:, columns].astype(jnp.float32)
        outs[4][rows, :] = (
            features[1, :, columns].astype(jnp.float32) * features[2, :, columns].astype(jnp.float32)
        )


def spread_acts(features, saved):
    flat = jax.ShapeDtypeStruct((saved.shape[0] * ROWS, LANES), jnp.float32)
    return pl.pallas_call(
        spread_kernel,
        in_specs=[VMEM] * 2,
        out_specs=[VMEM] * 5,
        out_shape=[flat] * 5,
        compiler_params=pltpu.CompilerParams(vmem_limit_bytes=GRANT),
        cost_estimate=SMALL,
        name="spread",
    )(features, saved)


def gate_kernel(at, has_acc, shards, count, halves, plan, *refs):
    acc = refs[0] if has_acc else None
    pieces = [
        jnp.concatenate([refs[has_acc + halves * i + part][...] for part in range(halves)])
        for i in range(count)
    ]
    weight, out, buffer, sems = refs[has_acc + halves * count:]
    width, deep = buffer.shape[1:]
    block = min(256, width)
    copies = []
    for shard in range(shards):
        columns = pl.ds(pl.multiple_of(plan[at + shard] * deep, deep), deep)
        copies.append(
            pltpu.make_async_copy(weight.at[:, columns], buffer.at[shard], sems.at[shard])
        )
        copies[-1].start()
    if shards < count:
        pieces = [jnp.where(plan[at + 1] > 0, *pieces)]
    elif shards > 1:
        pieces = [
            jnp.where(plan[at + shards + i] > 0, piece, jnp.zeros_like(piece))
            for i, piece in enumerate(pieces)
        ]
    for shard in range(shards):
        copies[shard].wait()
        for start in range(0, width, block):
            rows = pl.ds(start, block)
            value = lax.dot_general(
                pieces[shard], buffer[shard, rows, :], NT, preferred_element_type=jnp.float32
            )
            if shard:
                value = value + out[:, rows]
            elif has_acc:
                value = value + acc[:, rows]
            out[:, rows] = value


def gate_step(plan, at, acc, pieces, weight, shards):
    halves = len(pieces[0])
    tokens, deep = halves * pieces[0][0].shape[0], pieces[0][0].shape[1]
    width = weight.shape[0]
    has_acc = acc is not None
    flat = [piece for shard in pieces for piece in shard]
    return pl.pallas_call(
        functools.partial(gate_kernel, at, has_acc, shards, len(pieces), halves),
        in_specs=[SMEM] + [VMEM] * (has_acc + len(flat)) + [HBM],
        out_specs=VMEM,
        out_shape=jax.ShapeDtypeStruct((tokens, width), jnp.float32),
        scratch_shapes=[
            pltpu.VMEM((shards, width, deep), jnp.bfloat16),
            pltpu.SemaphoreType.DMA((shards,)),
        ],
        compiler_params=pltpu.CompilerParams(vmem_limit_bytes=GRANT),
        cost_estimate=SMALL,
        name="gate_step",
    )(plan, *([acc] if has_acc else []), *flat, weight)


def close_kernel(at, extra, late, plan, acc, piece, weight, query, saved, lam, other, *refs):
    if late:
        residues, (gconv, gquery, packet, products, gate) = other, refs
    else:
        later, (gconv, gquery, packet, gate) = other, refs
    tokens = piece.shape[0]
    first = tokens if late else 0
    width = weight.shape[0]
    poles = lam.shape[0]
    block = min(256, width)
    if width < ROWS * LANES:
        gate[...] = jnp.zeros(gate.shape, gate.dtype)
    arrived = jnp.where(plan[at] > 0, piece[...], jnp.zeros(piece.shape, piece.dtype))
    for start in range(0, width, block):
        columns = pl.ds(start, block)
        value = acc[pl.ds(first, tokens), columns] + lax.dot_general(
            arrived, weight[columns, :], NT, preferred_element_type=jnp.float32
        )
        for group in range(block // LANES):
            rows = pl.ds(start // LANES + group, tokens, stride=ROWS)
            gate[rows, :] = value[:, group * LANES:(group + 1) * LANES]

    def body(n, state):
        token = tokens - 1 - n
        here = tile(token)
        there = tile(first + token)
        grad = gate[here, :]
        conv = grad * query[there, :]
        gconv[here, :] = conv
        gquery[here, :] = grad * saved[there, :]
        state = tuple(lam[m] * state[m] + conv for m in range(poles))
        if late:
            products[here, :] = tree_sum([residues[m] * state[m] for m in range(poles)])
        return state

    if late:
        state = (jnp.zeros((ROWS, LANES), jnp.float32),) * poles
    else:
        state = tuple(later[m] for m in range(poles))
    state = lax.fori_loop(0, tokens, body, state, unroll=8)
    for m in range(poles):
        packet[m] = state[m]
    if not late:
        for row in range(extra - 1):
            packet[poles + row] = gconv[tile(row), :]
        for row in range(extra):
            packet[poles + extra - 1 + row] = gquery[tile(row), :]


def close_gate(plan, at, acc, piece, weight, query, saved, lam, extra, residues=None, later=None):
    tokens, deep = piece.shape
    width = weight.shape[0]
    poles = lam.shape[0]
    late = later is None
    flat = jax.ShapeDtypeStruct((tokens * ROWS, LANES), jnp.float32)
    packed = (poles if late else poles + 2 * extra - 1, ROWS, LANES)
    outs = [flat, flat, jax.ShapeDtypeStruct(packed, jnp.float32)] + [flat] * late
    return pl.pallas_call(
        functools.partial(close_kernel, at, extra, late),
        in_specs=[SMEM] + [VMEM] * 7,
        out_specs=[VMEM] * len(outs),
        out_shape=outs,
        scratch_shapes=[pltpu.VMEM(flat.shape, jnp.float32)],
        compiler_params=pltpu.CompilerParams(vmem_limit_bytes=GRANT),
        cost_estimate=SMALL,
        name="close_gate",
    )(plan, acc, piece, weight, query, saved, lam, residues if late else later)


def fold_kernel(plan, own, other, span, chip):
    poles = span.shape[0]
    first = plan[0] % 2 == 0
    for row in range(own.shape[0]):
        value = jnp.where(first, own[row], other[row])
        if row < poles:
            value = value + span[row] * jnp.where(first, other[row], own[row])
        chip[row] = value.astype(chip.dtype)


def fold(plan, own, other, span):
    return pl.pallas_call(
        fold_kernel,
        in_specs=[SMEM] + [VMEM] * 3,
        out_specs=VMEM,
        out_shape=jax.ShapeDtypeStruct(own.shape, jnp.bfloat16),
        compiler_params=pltpu.CompilerParams(vmem_limit_bytes=GRANT),
        cost_estimate=SMALL,
        name="fold",
    )(plan, own, other, span)


def filtered(filters, which, now, later):
    return tree_sum(
        [filters[which, 0] * now]
        + [filters[which, lag + 1] * value for lag, value in enumerate(later)]
    )


def gather_rows(spread, out, first, tokens):
    for group in range(out.shape[-1] // LANES):
        out[pl.ds(first, tokens), pl.ds(group * LANES, LANES)] = spread[
            pl.ds(first * ROWS + group, tokens, stride=ROWS), :
        ].astype(out.dtype)


def settle_kernel(
    taps, later, late_conv, late_query, early_conv, early_query, lam, residues, filters,
    products, passed, queries, spread,
):
    extra = taps - 1
    half = late_conv.shape[0] // ROWS
    poles = lam.shape[0]

    def late_body(n, after):
        token = half - TAIL - 1 - n
        now = late_query[tile(token), :]
        spread[tile(half + token), :] = filtered(filters, 0, now, after)
        return (now,) + after[:-1]

    after = tuple(late_query[tile(half - TAIL + row), :] for row in range(extra))
    after = lax.fori_loop(0, half - TAIL, late_body, after, unroll=8)

    def body(n, carry):
        state, after = carry
        here = tile(half - 1 - n)
        conv = early_conv[here, :]
        passed[here, :] = conv
        passed[tile(2 * half - 1 - n), :] = late_conv[here, :]
        state = tuple(lam[m] * state[m] + conv for m in range(poles))
        products[here, :] = tree_sum([residues[m] * state[m] for m in range(poles)])
        now = early_query[here, :]
        spread[here, :] = filtered(filters, 0, now, after)
        return state, (now,) + after[:-1]

    state = tuple(later[m] for m in range(poles))
    lax.fori_loop(0, half, body, (state, after), unroll=8)
    gather_rows(spread, queries, 0, 2 * half - TAIL)


def settle(later, late_conv, late_query, early_conv, early_query, lam, residues, filters, width):
    taps = filters.shape[1]
    half = late_conv.shape[0] // ROWS
    return pl.pallas_call(
        functools.partial(settle_kernel, taps),
        in_specs=[VMEM] * 8,
        out_specs=[VMEM] * 3,
        out_shape=[
            jax.ShapeDtypeStruct(early_conv.shape, jnp.float32),
            jax.ShapeDtypeStruct((2 * half * ROWS, LANES), jnp.float32),
            jax.ShapeDtypeStruct((2 * half, width), jnp.bfloat16),
        ],
        scratch_shapes=[pltpu.VMEM((2 * half * ROWS, LANES), jnp.float32)],
        compiler_params=pltpu.CompilerParams(vmem_limit_bytes=GRANT),
        cost_estimate=SMALL,
        name="settle",
    )(later, late_conv, late_query, early_conv, early_query, lam, residues, filters)


def scan_kernel(
    at_plan, taps, chips, plan, late_products, early_products, queries, late_query, key_acts,
    value_acts, lam, rate, residues, filters, kv_halo, own, other, *refs,
):
    arrived = refs[:chips - 1]
    weight, proj, chunk, chunk_rest, entering, spread, buffer, sem = refs[chips - 1:]
    extra = taps - 1
    tokens, width = proj.shape[1:]
    half = tokens // 2
    poles = lam.shape[0]
    rows = 2 * chunk.shape[0]
    copy = pltpu.make_async_copy(
        weight.at[:, pl.ds(pl.multiple_of(plan[at_plan] * rows, rows), rows), :], buffer, sem
    )
    copy.start()

    block = plan[0]
    core, here = block % 2, block // 2
    for m in range(poles):
        beyond = []
        for mask in range(1, chips):
            there = here ^ mask
            distance = (2 * tokens * jnp.maximum(there - here - 1, 0)).astype(jnp.float32)
            term = jnp.exp(-rate[m] * distance) * arrived[mask - 1][m].astype(jnp.float32)
            beyond.append(jnp.where(there > here, term, jnp.zeros_like(term)))
        beyond = tree_sum(beyond)
        entering[m] = jnp.where(
            core == 0, other[m] + jnp.exp(-rate[m] * tokens) * beyond, beyond
        )
    halo = []
    for row in range(poles, poles + 2 * extra - 1):
        value = jnp.where(core == 0, other[row], jnp.zeros_like(other[row]))
        for mask in range(1, chips):
            there = here ^ mask
            value = jnp.where(
                (core == 1) & (there == here + 1), arrived[mask - 1][row].astype(jnp.float32), value
            )
        halo.append(value)

    state = [entering[m] for m in range(poles)]
    parts = tuple(residues[m] * state[m] for m in range(poles))
    keys, values, after = [], [], []
    for row in range(extra):
        if row:
            state = [(state[m] - halo[row - 1]) * jnp.exp(rate[m]) for m in range(poles)]
        product = tree_sum([residues[m] * state[m] for m in range(poles)])
        keys.append(product * kv_halo[1, row])
        values.append(product * kv_halo[0, row])
        after.append(halo[extra - 1 + row])

    for token in range(tokens - 1, tokens - TAIL - 1, -1):
        now = late_query[pl.ds((token - half) * ROWS, ROWS), :]
        spread[0, pl.ds(token * ROWS, ROWS), :] = filtered(filters, 0, now, after)
        after = [now] + after[:-1]
    proj[0, pl.ds(0, tokens - TAIL), :] = queries[pl.ds(0, tokens - TAIL), :]
    gather_rows(spread.at[0], proj.at[0], tokens - TAIL, TAIL)

    def body(first, products, n, carry):
        parts, later = carry
        token = half - 1 - n
        at = tile(first + token)
        parts = tuple(lam[m] * parts[m] for m in range(poles))
        product = products[tile(token), :] + tree_sum(parts)
        now = (product * value_acts[at, :], product * key_acts[at, :])
        for which in range(2):
            spread[1 + which, at, :] = filtered(filters, 1 + which, now[which], later[which])
        return parts, tuple((now[which],) + later[which][:-1] for which in range(2))

    carry = (parts, (tuple(keys), tuple(values)))
    for first, products in ((half, late_products), (0, early_products)):
        carry = lax.fori_loop(0, half, functools.partial(body, first, products), carry, unroll=8)
    for which in range(1, 3):
        gather_rows(spread.at[which], proj.at[which], 0, tokens)
    copy.wait()
    project_rows(buffer, proj, (chunk, chunk_rest))


def scan_block(plan, at, settled, keys, values, lam, rate, residues, filters, kv_halo, own, other,
               arrived, weight, deep, width):
    tokens = keys.shape[0] // ROWS
    taps = filters.shape[1]
    return pl.pallas_call(
        functools.partial(scan_kernel, at, taps, len(arrived) + 1),
        in_specs=[SMEM] + [VMEM] * (13 + len(arrived)) + [HBM],
        out_specs=[VMEM] * 4,
        out_shape=[
            jax.ShapeDtypeStruct((3, tokens, width), jnp.bfloat16),
            jax.ShapeDtypeStruct((deep // 2, tokens), jnp.bfloat16),
            jax.ShapeDtypeStruct((deep // 2, tokens), jnp.bfloat16),
            jax.ShapeDtypeStruct(lam.shape, jnp.float32),
        ],
        scratch_shapes=[
            pltpu.VMEM((3, tokens * ROWS, LANES), jnp.float32),
            pltpu.VMEM((3, deep, width), jnp.bfloat16),
            pltpu.SemaphoreType.DMA,
        ],
        compiler_params=pltpu.CompilerParams(vmem_limit_bytes=GRANT),
        cost_estimate=SMALL,
        name="scan",
    )(plan, *settled, keys, values, lam, rate, residues, filters, kv_halo, own, other, *arrived, weight)


def project_rows(weight, proj, outs):
    rows = outs[0].shape[0]
    block = min(256, rows)
    for part, out in enumerate(outs):
        for start in range(0, rows, block):
            value = tree_sum([
                lax.dot_general(
                    weight[which, pl.ds(part * rows + start, block), :], proj[which],
                    NT, preferred_element_type=jnp.float32,
                )
                for which in range(3)
            ])
            out[pl.ds(start, block), :] = value.astype(out.dtype)


def add_up_residues(gconv, product, lam, entering, total):
    tokens = gconv.shape[0] // ROWS
    poles = lam.shape[0]

    def body(n, carry):
        state, sums = carry
        at = tile(tokens - 1 - n)
        conv, both = gconv[at, :], product[at, :]
        state = tuple(lam[m] * state[m] + conv for m in range(poles))
        return state, tuple(sums[m] + both * state[m] for m in range(poles))

    state = tuple(entering[m] for m in range(poles))
    zero = jnp.zeros((ROWS, LANES), jnp.float32)
    _, sums = lax.fori_loop(0, tokens, body, (state, (zero,) * poles), unroll=8)
    for m in range(poles):
        total[m] = sums[m]


def project_kernel(at, count, sources, plan, proj, weight, *refs):
    if sources:
        add_up = functools.partial(add_up_residues, *refs[:sources + 1])
        refs = refs[sources + 1:]
    outs, (buffer, sems) = refs[:2 * count], refs[2 * count:]
    deep = buffer.shape[2]
    copies = []
    for i in range(count):
        start = pl.multiple_of(plan[at + i] * deep, deep)
        copies.append(
            pltpu.make_async_copy(weight.at[:, pl.ds(start, deep), :], buffer.at[i], sems.at[i])
        )
        copies[-1].start()
    if sources:
        add_up()
    for i in range(count):
        copies[i].wait()
        project_rows(buffer.at[i], proj, outs[2 * i:2 * i + 2])


def project(plan, at, count, proj, weight, deep, sources=()):
    _, tokens, width = proj.shape
    outs = [jax.ShapeDtypeStruct((deep // 2, tokens), jnp.bfloat16)] * (2 * count)
    if sources:
        outs = [jax.ShapeDtypeStruct(sources[-1].shape, jnp.float32)] + outs
    return pl.pallas_call(
        functools.partial(project_kernel, at, count, len(sources)),
        in_specs=[SMEM, VMEM, HBM] + [VMEM] * len(sources),
        out_specs=[VMEM] * len(outs),
        out_shape=outs,
        scratch_shapes=[
            pltpu.VMEM((count, 3, deep, width), jnp.bfloat16),
            pltpu.SemaphoreType.DMA((count,)),
        ],
        compiler_params=pltpu.CompilerParams(vmem_limit_bytes=GRANT),
        cost_estimate=pl.CostEstimate(
            flops=6 * tokens * width * deep * count,
            bytes_accessed=6 * width * deep * count,
            transcendentals=0,
        ),
        name="project",
    )(plan, proj, weight, *sources)


def scalars(*values):
    return jnp.stack([jnp.asarray(value, jnp.int32) for value in values])


def tiles(array):
    lead = array.shape[:-1]
    groups = array.shape[-1] // LANES
    array = array.reshape(lead + (groups, LANES))
    if groups < ROWS:
        array = jnp.pad(array, [(0, 0)] * len(lead) + [(0, ROWS - groups), (0, 0)])
    return array


def swap_even(value, count):
    return lax.ppermute(value, "chan", [(i, i ^ 1) for i in range(count)])


def swap_odd(value, count, blocks):
    pairs = []
    for block in range(blocks):
        for i in range(count):
            other = i + 1 if i % 2 else i - 1
            if 0 <= other < count:
                pairs.append((block * count + i, block * count + other))
            else:
                pairs.append((block * count + i, (block ^ 1) * count + i))
    return lax.ppermute(value, ("ctx", "chan"), pairs)


def swap_ctx(value, mask, blocks):
    return lax.ppermute(value, "ctx", [(i, i ^ mask) for i in range(blocks)])


def tie(*values):
    return lax.optimization_barrier(values)


def local(features, saved_conv, grad_out, out_weight, in_weight, short_taps, residues, decay_time):
    f32, bf16 = jnp.float32, jnp.bfloat16
    tokens, width = saved_conv.shape
    taps = short_taps.shape[1]
    extra = taps - 1
    poles = residues.shape[0]
    count = lax.axis_size("chan")
    me = lax.axis_index("chan")
    even = me % 2 == 0
    deep = in_weight.shape[1] // count
    blocks = lax.axis_size("ctx")
    block = lax.axis_index("ctx")

    rate = tiles(1.0 / decay_time)
    lam = jnp.exp(-rate)
    span = jnp.exp(-rate * tokens)
    res = tiles(residues)
    filters = tiles(short_taps)

    def shared(phase):
        far = count - phase
        as_even = jnp.where(me < phase, me + far, jnp.maximum(me - far + 1, 0))
        as_odd = jnp.where(me >= far, me - far, jnp.minimum(me + far - 1, count - 1))
        return jnp.where(even, as_even, as_odd)

    def reached(phase, along):
        right = jnp.minimum(me + count - phase, count - 1)
        left = jnp.maximum(me - (count - phase), 0)
        return jnp.where(along, right, left)

    def shards(phase):
        above, below = me + phase, me - phase
        high, low = jnp.minimum(above, count - 1), jnp.maximum(below, 0)
        at_even, at_odd = jnp.where(even, high, low), jnp.where(even, low, high)
        even_ok = jnp.where(even, above < count, below >= 0)
        odd_ok = jnp.where(even, below >= 0, above < count)
        if 2 * phase == count:
            return [jnp.where(even_ok, at_even, at_odd), even_ok]
        return [at_even, at_odd, even_ok, odd_ok]

    edge = (me == 0) | (me == count - 1)
    plan, places = [block, edge], {}

    def planned(name, values):
        places[name] = len(plan)
        plan.extend(values)

    planned("own", [me, 1])
    for phase in range(1, count - 1):
        planned(("gate", phase), shards(phase))
    planned("first", [shared(1)])
    chunks = []
    for phase in range(2, count):
        if 2 * phase <= count:
            chunks.append(shared(phase))
        else:
            chunks.append(reached(phase, even))
            if phase + 1 < count:
                chunks.append(reached(phase + 1, ~even))
    chunks.append(me)
    planned("chunks", chunks)
    plan = scalars(*plan)

    half = tokens // 2
    evens = [swap_even(grad_out[half:], count)]
    odds = [swap_odd(grad_out[half:], count, blocks)]
    rest, plan, rate, lam, span, res, filters = tie(grad_out, plan, rate, lam, span, res, filters)
    evens.append(swap_even(rest[:half], count))
    odds.append(swap_odd(rest[:half], count, blocks))
    evens[0], odds[0] = tie(evens[0], odds[0])
    acc = None
    for phase in range(1, count - 1):
        ahead = [[swap_even(odds[0], count)], [swap_odd(evens[0], count, blocks)]]
        if phase == 1:
            acc = gate_step(plan, places["own"], None, [[grad_out]], out_weight, 1)
            evens[1], odds[1], acc = tie(evens[1], odds[1], acc)
        ahead[0].append(swap_even(odds[1], count))
        ahead[1].append(swap_odd(evens[1], count, blocks))
        acc = gate_step(
            plan, places["gate", phase], acc, [evens[::-1], odds[::-1]], out_weight,
            1 if 2 * phase == count else 2,
        )
        evens, odds = ahead
        if phase < count - 2:
            evens[0], odds[0], acc = tie(evens[0], odds[0], acc)
            evens[1], odds[1] = tie(evens[1], odds[1])
        if phase == 1:
            odds[0], features, saved_conv = tie(odds[0], features, saved_conv)
            kv_halo = tiles(features[1:3, :extra].astype(f32))
            kv_halo = lax.ppermute(kv_halo, "ctx", [(i, (i - 1) % blocks) for i in range(blocks)])
            last = jnp.where(
                even, jnp.minimum(count - 1, me + count - 1), jnp.maximum(me - count + 1, 0)
            )
            last_weight = lax.dynamic_slice(out_weight, (0, last * width), (width, width))
            query, keys, values, saved, product = spread_acts(features, saved_conv)
            odds[1], kv_halo, last_weight, query, keys, values, saved, product = tie(
                odds[1], kv_halo, last_weight, query, keys, values, saved, product
            )
    late_conv, late_query, later, late_products = close_gate(
        plan, 1, acc, evens[0], last_weight, query, saved, lam, extra, residues=res
    )
    early_conv, early_query, packet = close_gate(
        plan, 1, acc, evens[1], last_weight, query, saved, lam, extra, later=later
    )

    other = swap_ctx(packet, 1, blocks)
    chip = fold(plan, packet, other, span)
    arrived = [swap_ctx(chip, 2 * mask, blocks) for mask in range(1, blocks // 2)]
    early_products, gconv, queries = settle(
        later, late_conv, late_query, early_conv, early_query, lam, res, filters, width
    )

    def added(*parts):
        return sum(value.astype(f32) for value in parts if value is not None).astype(bf16)

    def masked(value):
        return None if value is None else jnp.where(edge, jnp.zeros_like(value), value)

    proj, *part, entering = scan_block(
        plan, places["first"], [late_products, early_products, queries, late_query], keys, values,
        lam, rate, res, filters, kv_halo, packet, other, arrived, in_weight, deep, width,
    )
    total, *parts = project(
        plan, places["chunks"], 1, proj, in_weight, deep, [gconv, product, lam, entering]
    )
    for_even, for_odd = {1: part}, {2: part}
    evens, odds = [swap_even(piece, count) for piece in part], [None, None]
    evens[0], proj, total, *parts = tie(
        evens[0], proj, total, *parts
    )
    parts += project(plan, places["chunks"] + 1, len(chunks) - 1, proj, in_weight, deep)
    for phase in range(2, count):
        for_even[phase], parts = parts[:2], parts[2:]
        if 2 * phase <= count:
            for_odd[phase + 1] = for_even[phase]
        elif phase + 1 < count:
            for_odd[phase + 1], parts = parts[:2], parts[2:]
    for phase in range(2, count):
        if phase > 2:
            for piece in range(2):
                evens[piece], odds[piece] = tie(evens[piece], odds[piece])
        if phase == count - 1:
            odds[0], total = tie(odds[0], total)
        for piece in range(2):
            next_even = swap_even(added(for_even[phase][piece], masked(odds[piece])), count)
            odds[piece] = swap_odd(added(for_odd[phase][piece], evens[piece]), count, blocks)
            evens[piece] = next_even
    grad_input = jnp.concatenate(
        [added(parts[piece], evens[piece], masked(odds[piece])) for piece in range(2)]
    )

    mask = 1
    while mask < blocks:
        total = total + swap_ctx(total, mask, blocks)
        mask *= 2
    grad_residue = total[:, :width // LANES].reshape(poles, width) / (tokens * blocks)
    return grad_input, grad_residue


def solution(mesh):
    return jax.shard_map(
        local,
        mesh=mesh,
        in_specs=(
            P(None, "ctx", "chan"),
            P("ctx", "chan"),
            P("ctx", "chan"),
            P("chan", None),
            P(None, None, "chan"),
            P(None, None, "chan"),
            P(None, "chan"),
            P(None, "chan"),
        ),
        out_specs=(P("chan", "ctx"), P(None, "chan")),
        check_vma=False,
    )
```

```python
import functools

import jax
import jax.numpy as jnp
from jax import lax
from jax.experimental import pallas as pl
from jax.experimental.pallas import tpu as pltpu
from jax.sharding import PartitionSpec as P

LANES = 128
ROWS = 8
NT = (((1,), (1,)), ((), ()))
VMEM = pl.BlockSpec(memory_space=pltpu.VMEM)
HBM = pl.BlockSpec(memory_space=pltpu.HBM)
SMEM = pl.BlockSpec(memory_space=pltpu.SMEM)
GRANT = 46 * 2**20
TAIL = 16
SMALL = pl.CostEstimate(flops=1, bytes_accessed=1, transcendentals=0)


def tile(token):
    return pl.ds(pl.multiple_of(token * ROWS, ROWS), ROWS)


def tree_sum(terms):
    terms = list(terms)
    while len(terms) > 1:
        paired = [a + b for a, b in zip(terms[::2], terms[1::2])]
        terms = paired + terms[2 * len(paired):]
    return terms[0]


def spread_kernel(features, saved, *outs):
    tokens, width = saved.shape
    if width < ROWS * LANES:
        for out in outs:
            out[...] = jnp.zeros(out.shape, out.dtype)
    for group in range(width // LANES):
        columns = pl.ds(group * LANES, LANES)
        rows = pl.ds(group, tokens, stride=ROWS)
        for which in range(3):
            outs[which][rows, :] = features[which, :, columns].astype(jnp.float32)
        outs[3][rows, :] = saved[:, columns].astype(jnp.float32)
        outs[4][rows, :] = (
            features[1, :, columns].astype(jnp.float32) * features[2, :, columns].astype(jnp.float32)
        )


def spread_acts(features, saved):
    flat = jax.ShapeDtypeStruct((saved.shape[0] * ROWS, LANES), jnp.float32)
    return pl.pallas_call(
        spread_kernel,
        in_specs=[VMEM] * 2,
        out_specs=[VMEM] * 5,
        out_shape=[flat] * 5,
        compiler_params=pltpu.CompilerParams(vmem_limit_bytes=GRANT),
        cost_estimate=SMALL,
        name="spread",
    )(features, saved)


def gate_kernel(at, has_acc, shards, count, halves, plan, *refs):
    acc = refs[0] if has_acc else None
    pieces = [
        jnp.concatenate([refs[has_acc + halves * i + part][...] for part in range(halves)])
        for i in range(count)
    ]
    weight, out, buffer, sems = refs[has_acc + halves * count:]
    width, deep = buffer.shape[1:]
    block = min(256, width)
    copies = []
    for shard in range(shards):
        columns = pl.ds(pl.multiple_of(plan[at + shard] * deep, deep), deep)
        copies.append(
            pltpu.make_async_copy(weight.at[:, columns], buffer.at[shard], sems.at[shard])
        )
        copies[-1].start()
    if shards < count:
        pieces = [jnp.where(plan[at + 1] > 0, *pieces)]
    elif shards > 1:
        pieces = [
            jnp.where(plan[at + shards + i] > 0, piece, jnp.zeros_like(piece))
            for i, piece in enumerate(pieces)
        ]
    for shard in range(shards):
        copies[shard].wait()
        for start in range(0, width, block):
            rows = pl.ds(start, block)
            value = lax.dot_general(
                pieces[shard], buffer[shard, rows, :], NT, preferred_element_type=jnp.float32
            )
            if shard:
                value = value + out[:, rows]
            elif has_acc:
                value = value + acc[:, rows]
            out[:, rows] = value


def gate_step(plan, at, acc, pieces, weight, shards):
    halves = len(pieces[0])
    tokens, deep = halves * pieces[0][0].shape[0], pieces[0][0].shape[1]
    width = weight.shape[0]
    has_acc = acc is not None
    flat = [piece for shard in pieces for piece in shard]
    return pl.pallas_call(
        functools.partial(gate_kernel, at, has_acc, shards, len(pieces), halves),
        in_specs=[SMEM] + [VMEM] * (has_acc + len(flat)) + [HBM],
        out_specs=VMEM,
        out_shape=jax.ShapeDtypeStruct((tokens, width), jnp.float32),
        scratch_shapes=[
            pltpu.VMEM((shards, width, deep), jnp.bfloat16),
            pltpu.SemaphoreType.DMA((shards,)),
        ],
        compiler_params=pltpu.CompilerParams(vmem_limit_bytes=GRANT),
        cost_estimate=SMALL,
        name="gate_step",
    )(plan, *([acc] if has_acc else []), *flat, weight)


def close_kernel(at, extra, late, plan, acc, piece, weight, query, saved, lam, other, *refs):
    if late:
        residues, (gconv, gquery, packet, products, gate) = other, refs
    else:
        later, (gconv, gquery, packet, gate) = other, refs
    tokens = piece.shape[0]
    first = tokens if late else 0
    width = weight.shape[0]
    poles = lam.shape[0]
    block = min(256, width)
    if width < ROWS * LANES:
        gate[...] = jnp.zeros(gate.shape, gate.dtype)
    arrived = jnp.where(plan[at] > 0, piece[...], jnp.zeros(piece.shape, piece.dtype))
    for start in range(0, width, block):
        columns = pl.ds(start, block)
        value = acc[pl.ds(first, tokens), columns] + lax.dot_general(
            arrived, weight[columns, :], NT, preferred_element_type=jnp.float32
        )
        for group in range(block // LANES):
            rows = pl.ds(start // LANES + group, tokens, stride=ROWS)
            gate[rows, :] = value[:, group * LANES:(group + 1) * LANES]

    def body(n, state):
        token = tokens - 1 - n
        here = tile(token)
        there = tile(first + token)
        grad = gate[here, :]
        conv = grad * query[there, :]
        gconv[here, :] = conv
        gquery[here, :] = grad * saved[there, :]
        state = tuple(lam[m] * state[m] + conv for m in range(poles))
        if late:
            products[here, :] = tree_sum([residues[m] * state[m] for m in range(poles)])
        return state

    if late:
        state = (jnp.zeros((ROWS, LANES), jnp.float32),) * poles
    else:
        state = tuple(later[m] for m in range(poles))
    state = lax.fori_loop(0, tokens, body, state, unroll=8)
    for m in range(poles):
        packet[m] = state[m]
    if not late:
        for row in range(extra - 1):
            packet[poles + row] = gconv[tile(row), :]
        for row in range(extra):
            packet[poles + extra - 1 + row] = gquery[tile(row), :]


def close_gate(plan, at, acc, piece, weight, query, saved, lam, extra, residues=None, later=None):
    tokens, deep = piece.shape
    width = weight.shape[0]
    poles = lam.shape[0]
    late = later is None
    flat = jax.ShapeDtypeStruct((tokens * ROWS, LANES), jnp.float32)
    packed = (poles if late else poles + 2 * extra - 1, ROWS, LANES)
    outs = [flat, flat, jax.ShapeDtypeStruct(packed, jnp.float32)] + [flat] * late
    return pl.pallas_call(
        functools.partial(close_kernel, at, extra, late),
        in_specs=[SMEM] + [VMEM] * 7,
        out_specs=[VMEM] * len(outs),
        out_shape=outs,
        scratch_shapes=[pltpu.VMEM(flat.shape, jnp.float32)],
        compiler_params=pltpu.CompilerParams(vmem_limit_bytes=GRANT),
        cost_estimate=SMALL,
        name="close_gate",
    )(plan, acc, piece, weight, query, saved, lam, residues if late else later)


def fold_kernel(plan, own, other, span, chip):
    poles = span.shape[0]
    first = plan[0] % 2 == 0
    for row in range(own.shape[0]):
        value = jnp.where(first, own[row], other[row])
        if row < poles:
            value = value + span[row] * jnp.where(first, other[row], own[row])
        chip[row] = value.astype(chip.dtype)


def fold(plan, own, other, span):
    return pl.pallas_call(
        fold_kernel,
        in_specs=[SMEM] + [VMEM] * 3,
        out_specs=VMEM,
        out_shape=jax.ShapeDtypeStruct(own.shape, jnp.float32),
        compiler_params=pltpu.CompilerParams(vmem_limit_bytes=GRANT),
        cost_estimate=SMALL,
        name="fold",
    )(plan, own, other, span)


def filtered(filters, which, now, later):
    return tree_sum(
        [filters[which, 0] * now]
        + [filters[which, lag + 1] * value for lag, value in enumerate(later)]
    )


def gather_rows(spread, out, first, tokens):
    for group in range(out.shape[-1] // LANES):
        out[pl.ds(first, tokens), pl.ds(group * LANES, LANES)] = spread[
            pl.ds(first * ROWS + group, tokens, stride=ROWS), :
        ].astype(out.dtype)


def settle_kernel(
    taps, later, late_conv, late_query, early_conv, early_query, lam, residues, filters,
    products, passed, queries, spread,
):
    extra = taps - 1
    half = late_conv.shape[0] // ROWS
    poles = lam.shape[0]

    def late_body(n, after):
        token = half - TAIL - 1 - n
        now = late_query[tile(token), :]
        spread[tile(half + token), :] = filtered(filters, 0, now, after)
        return (now,) + after[:-1]

    after = tuple(late_query[tile(half - TAIL + row), :] for row in range(extra))
    after = lax.fori_loop(0, half - TAIL, late_body, after, unroll=8)

    def body(n, carry):
        state, after = carry
        here = tile(half - 1 - n)
        conv = early_conv[here, :]
        passed[here, :] = conv
        passed[tile(2 * half - 1 - n), :] = late_conv[here, :]
        state = tuple(lam[m] * state[m] + conv for m in range(poles))
        products[here, :] = tree_sum([residues[m] * state[m] for m in range(poles)])
        now = early_query[here, :]
        spread[here, :] = filtered(filters, 0, now, after)
        return state, (now,) + after[:-1]

    state = tuple(later[m] for m in range(poles))
    lax.fori_loop(0, half, body, (state, after), unroll=8)
    gather_rows(spread, queries, 0, 2 * half - TAIL)


def settle(later, late_conv, late_query, early_conv, early_query, lam, residues, filters, width):
    taps = filters.shape[1]
    half = late_conv.shape[0] // ROWS
    return pl.pallas_call(
        functools.partial(settle_kernel, taps),
        in_specs=[VMEM] * 8,
        out_specs=[VMEM] * 3,
        out_shape=[
            jax.ShapeDtypeStruct(early_conv.shape, jnp.float32),
            jax.ShapeDtypeStruct((2 * half * ROWS, LANES), jnp.float32),
            jax.ShapeDtypeStruct((2 * half, width), jnp.bfloat16),
        ],
        scratch_shapes=[pltpu.VMEM((2 * half * ROWS, LANES), jnp.float32)],
        compiler_params=pltpu.CompilerParams(vmem_limit_bytes=GRANT),
        cost_estimate=SMALL,
        name="settle",
    )(later, late_conv, late_query, early_conv, early_query, lam, residues, filters)


def scan_kernel(
    at_plan, taps, chips, plan, late_products, early_products, queries, late_query, key_acts,
    value_acts, lam, rate, residues, filters, kv_halo, own, other, *refs,
):
    arrived = refs[:chips - 1]
    weight, proj, chunk, chunk_rest, entering, spread, buffer, sem = refs[chips - 1:]
    extra = taps - 1
    tokens, width = proj.shape[1:]
    half = tokens // 2
    poles = lam.shape[0]
    rows = 2 * chunk.shape[0]
    copy = pltpu.make_async_copy(
        weight.at[:, pl.ds(pl.multiple_of(plan[at_plan] * rows, rows), rows), :], buffer, sem
    )
    copy.start()

    block = plan[0]
    core, here = block % 2, block // 2
    for m in range(poles):
        beyond = []
        for mask in range(1, chips):
            there = here ^ mask
            distance = (2 * tokens * jnp.maximum(there - here - 1, 0)).astype(jnp.float32)
            term = jnp.exp(-rate[m] * distance) * arrived[mask - 1][m].astype(jnp.float32)
            beyond.append(jnp.where(there > here, term, jnp.zeros_like(term)))
        beyond = tree_sum(beyond)
        entering[m] = jnp.where(
            core == 0, other[m] + jnp.exp(-rate[m] * tokens) * beyond, beyond
        )
    halo = []
    for row in range(poles, poles + 2 * extra - 1):
        value = jnp.where(core == 0, other[row], jnp.zeros_like(other[row]))
        for mask in range(1, chips):
            there = here ^ mask
            value = jnp.where(
                (core == 1) & (there == here + 1), arrived[mask - 1][row].astype(jnp.float32), value
            )
        halo.append(value)

    state = [entering[m] for m in range(poles)]
    parts = tuple(residues[m] * state[m] for m in range(poles))
    keys, values, after = [], [], []
    for row in range(extra):
        if row:
            state = [(state[m] - halo[row - 1]) * jnp.exp(rate[m]) for m in range(poles)]
        product = tree_sum([residues[m] * state[m] for m in range(poles)])
        keys.append(product * kv_halo[1, row])
        values.append(product * kv_halo[0, row])
        after.append(halo[extra - 1 + row])

    for token in range(tokens - 1, tokens - TAIL - 1, -1):
        now = late_query[pl.ds((token - half) * ROWS, ROWS), :]
        spread[0, pl.ds(token * ROWS, ROWS), :] = filtered(filters, 0, now, after)
        after = [now] + after[:-1]
    proj[0, pl.ds(0, tokens - TAIL), :] = queries[pl.ds(0, tokens - TAIL), :]
    gather_rows(spread.at[0], proj.at[0], tokens - TAIL, TAIL)

    def body(first, products, n, carry):
        parts, later = carry
        token = half - 1 - n
        at = tile(first + token)
        parts = tuple(lam[m] * parts[m] for m in range(poles))
        product = products[tile(token), :] + tree_sum(parts)
        now = (product * value_acts[at, :], product * key_acts[at, :])
        for which in range(2):
            spread[1 + which, at, :] = filtered(filters, 1 + which, now[which], later[which])
        return parts, tuple((now[which],) + later[which][:-1] for which in range(2))

    carry = (parts, (tuple(keys), tuple(values)))
    for first, products in ((half, late_products), (0, early_products)):
        carry = lax.fori_loop(0, half, functools.partial(body, first, products), carry, unroll=8)
    for which in range(1, 3):
        gather_rows(spread.at[which], proj.at[which], 0, tokens)
    copy.wait()
    project_rows(buffer, proj, (chunk, chunk_rest))


def scan_block(plan, at, settled, keys, values, lam, rate, residues, filters, kv_halo, own, other,
               arrived, weight, deep, width):
    tokens = keys.shape[0] // ROWS
    taps = filters.shape[1]
    return pl.pallas_call(
        functools.partial(scan_kernel, at, taps, len(arrived) + 1),
        in_specs=[SMEM] + [VMEM] * (13 + len(arrived)) + [HBM],
        out_specs=[VMEM] * 4,
        out_shape=[
            jax.ShapeDtypeStruct((3, tokens, width), jnp.bfloat16),
            jax.ShapeDtypeStruct((deep // 2, tokens), jnp.bfloat16),
            jax.ShapeDtypeStruct((deep // 2, tokens), jnp.bfloat16),
            jax.ShapeDtypeStruct(lam.shape, jnp.float32),
        ],
        scratch_shapes=[
            pltpu.VMEM((3, tokens * ROWS, LANES), jnp.float32),
            pltpu.VMEM((3, deep, width), jnp.bfloat16),
            pltpu.SemaphoreType.DMA,
        ],
        compiler_params=pltpu.CompilerParams(vmem_limit_bytes=GRANT),
        cost_estimate=SMALL,
        name="scan",
    )(plan, *settled, keys, values, lam, rate, residues, filters, kv_halo, own, other, *arrived, weight)


def project_rows(weight, proj, outs):
    rows = outs[0].shape[0]
    block = min(256, rows)
    for part, out in enumerate(outs):
        for start in range(0, rows, block):
            value = tree_sum([
                lax.dot_general(
                    weight[which, pl.ds(part * rows + start, block), :], proj[which],
                    NT, preferred_element_type=jnp.float32,
                )
                for which in range(3)
            ])
            out[pl.ds(start, block), :] = value.astype(out.dtype)


def add_up_residues(tiles_of, gconv, product, lam, entering, total):
    tokens = gconv.shape[0] // ROWS
    poles = lam.shape[0]

    def body(n, carry):
        state, sums = carry
        at = tile(tokens - 1 - n)
        conv, both = gconv[at, :], product[at, :]
        state = tuple(lam[m] * state[m] + conv for m in range(poles))
        return state, tuple(sums[m] + both * state[m] for m in range(poles))

    state = tuple(entering[m] for m in range(poles))
    zero = jnp.zeros((ROWS, LANES), jnp.float32)
    _, sums = lax.fori_loop(0, tokens, body, (state, (zero,) * poles), unroll=8)
    for m in range(poles):
        tiles_of[pl.ds(m * ROWS, ROWS), :] = sums[m]
    gather_rows(tiles_of, total, 0, poles)


def project_kernel(at, count, sources, plan, proj, weight, *refs):
    if sources:
        add_up = functools.partial(add_up_residues, refs[-1], *refs[:sources + 1])
        refs = refs[sources + 1:-1]
    outs, (buffer, sems) = refs[:2 * count], refs[2 * count:]
    deep = buffer.shape[2]
    copies = []
    for i in range(count):
        start = pl.multiple_of(plan[at + i] * deep, deep)
        copies.append(
            pltpu.make_async_copy(weight.at[:, pl.ds(start, deep), :], buffer.at[i], sems.at[i])
        )
        copies[-1].start()
    if sources:
        add_up()
    for i in range(count):
        copies[i].wait()
        project_rows(buffer.at[i], proj, outs[2 * i:2 * i + 2])


def project(plan, at, count, proj, weight, deep, sources=()):
    _, tokens, width = proj.shape
    outs = [jax.ShapeDtypeStruct((deep // 2, tokens), jnp.bfloat16)] * (2 * count)
    if sources:
        outs = [jax.ShapeDtypeStruct((sources[-1].shape[0], width), jnp.float32)] + outs
    return pl.pallas_call(
        functools.partial(project_kernel, at, count, len(sources)),
        in_specs=[SMEM, VMEM, HBM] + [VMEM] * len(sources),
        out_specs=[VMEM] * len(outs),
        out_shape=outs,
        scratch_shapes=[
            pltpu.VMEM((count, 3, deep, width), jnp.bfloat16),
            pltpu.SemaphoreType.DMA((count,)),
        ] + [pltpu.VMEM((array.shape[0] * ROWS, LANES), jnp.float32) for array in sources[-1:]],
        compiler_params=pltpu.CompilerParams(vmem_limit_bytes=GRANT),
        cost_estimate=pl.CostEstimate(
            flops=6 * tokens * width * deep * count,
            bytes_accessed=6 * width * deep * count,
            transcendentals=0,
        ),
        name="project",
    )(plan, proj, weight, *sources)


def scalars(*values):
    return jnp.stack([jnp.asarray(value, jnp.int32) for value in values])


def tiles(array):
    lead = array.shape[:-1]
    groups = array.shape[-1] // LANES
    array = array.reshape(lead + (groups, LANES))
    if groups < ROWS:
        array = jnp.pad(array, [(0, 0)] * len(lead) + [(0, ROWS - groups), (0, 0)])
    return array


def swap_even(value, count):
    return lax.ppermute(value, "chan", [(i, i ^ 1) for i in range(count)])


def swap_odd(value, count, blocks):
    pairs = []
    for block in range(blocks):
        for i in range(count):
            other = i + 1 if i % 2 else i - 1
            if 0 <= other < count:
                pairs.append((block * count + i, block * count + other))
            else:
                pairs.append((block * count + i, (block ^ 1) * count + i))
    return lax.ppermute(value, ("ctx", "chan"), pairs)


def swap_ctx(value, mask, blocks):
    return lax.ppermute(value, "ctx", [(i, i ^ mask) for i in range(blocks)])


def tie(*values):
    return lax.optimization_barrier(values)


def local(features, saved_conv, grad_out, out_weight, in_weight, short_taps, residues, decay_time):
    f32, bf16 = jnp.float32, jnp.bfloat16
    tokens, width = saved_conv.shape
    taps = short_taps.shape[1]
    extra = taps - 1
    poles = residues.shape[0]
    count = lax.axis_size("chan")
    me = lax.axis_index("chan")
    even = me % 2 == 0
    deep = in_weight.shape[1] // count
    blocks = lax.axis_size("ctx")
    block = lax.axis_index("ctx")

    rate = tiles(1.0 / decay_time)
    lam = jnp.exp(-rate)
    span = jnp.exp(-rate * tokens)
    res = tiles(residues)
    filters = tiles(short_taps)

    def shared(phase):
        far = count - phase
        as_even = jnp.where(me < phase, me + far, jnp.maximum(me - far + 1, 0))
        as_odd = jnp.where(me >= far, me - far, jnp.minimum(me + far - 1, count - 1))
        return jnp.where(even, as_even, as_odd)

    def reached(phase, along):
        right = jnp.minimum(me + count - phase, count - 1)
        left = jnp.maximum(me - (count - phase), 0)
        return jnp.where(along, right, left)

    def shards(phase):
        above, below = me + phase, me - phase
        high, low = jnp.minimum(above, count - 1), jnp.maximum(below, 0)
        at_even, at_odd = jnp.where(even, high, low), jnp.where(even, low, high)
        even_ok = jnp.where(even, above < count, below >= 0)
        odd_ok = jnp.where(even, below >= 0, above < count)
        if 2 * phase == count:
            return [jnp.where(even_ok, at_even, at_odd), even_ok]
        return [at_even, at_odd, even_ok, odd_ok]

    edge = (me == 0) | (me == count - 1)
    plan, places = [block, edge], {}

    def planned(name, values):
        places[name] = len(plan)
        plan.extend(values)

    planned("own", [me, 1])
    for phase in range(1, count - 1):
        planned(("gate", phase), shards(phase))
    planned("first", [shared(1)])
    chunks = []
    for phase in range(2, count):
        if 2 * phase <= count:
            chunks.append(shared(phase))
        else:
            chunks.append(reached(phase, even))
            if phase + 1 < count:
                chunks.append(reached(phase + 1, ~even))
    chunks.append(me)
    planned("chunks", chunks)
    plan = scalars(*plan)

    half = tokens // 2
    evens = [swap_even(grad_out[half:], count)]
    odds = [swap_odd(grad_out[half:], count, blocks)]
    rest, plan, rate, lam, span, res, filters = tie(grad_out, plan, rate, lam, span, res, filters)
    evens.append(swap_even(rest[:half], count))
    odds.append(swap_odd(rest[:half], count, blocks))
    evens[0], odds[0] = tie(evens[0], odds[0])
    acc = None
    for phase in range(1, count - 1):
        ahead = [[swap_even(odds[0], count)], [swap_odd(evens[0], count, blocks)]]
        if phase == 1:
            acc = gate_step(plan, places["own"], None, [[grad_out]], out_weight, 1)
            evens[1], odds[1], acc = tie(evens[1], odds[1], acc)
        ahead[0].append(swap_even(odds[1], count))
        ahead[1].append(swap_odd(evens[1], count, blocks))
        acc = gate_step(
            plan, places["gate", phase], acc, [evens[::-1], odds[::-1]], out_weight,
            1 if 2 * phase == count else 2,
        )
        evens, odds = ahead
        if phase < count - 2:
            evens[0], odds[0], acc = tie(evens[0], odds[0], acc)
            evens[1], odds[1] = tie(evens[1], odds[1])
        if phase == 1:
            odds[0], features, saved_conv = tie(odds[0], features, saved_conv)
            kv_halo = tiles(features[1:3, :extra].astype(f32))
            kv_halo = lax.ppermute(kv_halo, "ctx", [(i, (i - 1) % blocks) for i in range(blocks)])
            last = jnp.where(
                even, jnp.minimum(count - 1, me + count - 1), jnp.maximum(me - count + 1, 0)
            )
            last_weight = lax.dynamic_slice(out_weight, (0, last * width), (width, width))
            query, keys, values, saved, product = spread_acts(features, saved_conv)
            odds[1], kv_halo, last_weight, query, keys, values, saved, product = tie(
                odds[1], kv_halo, last_weight, query, keys, values, saved, product
            )
    late_conv, late_query, later, late_products = close_gate(
        plan, 1, acc, evens[0], last_weight, query, saved, lam, extra, residues=res
    )
    early_conv, early_query, packet = close_gate(
        plan, 1, acc, evens[1], last_weight, query, saved, lam, extra, later=later
    )

    other = swap_ctx(packet, 1, blocks)
    chip = fold(plan, packet, other, span)
    arrived = [swap_ctx(chip, 2 * mask, blocks) for mask in range(1, blocks // 2)]
    early_products, gconv, queries = settle(
        later, late_conv, late_query, early_conv, early_query, lam, res, filters, width
    )

    def added(*parts):
        return sum(value.astype(f32) for value in parts if value is not None).astype(bf16)

    def masked(value):
        return None if value is None else jnp.where(edge, jnp.zeros_like(value), value)

    proj, *part, entering = scan_block(
        plan, places["first"], [late_products, early_products, queries, late_query], keys, values,
        lam, rate, res, filters, kv_halo, packet, other, arrived, in_weight, deep, width,
    )
    total, *parts = project(
        plan, places["chunks"], 1, proj, in_weight, deep, [gconv, product, lam, entering]
    )
    for_even, for_odd = {1: part}, {2: part}
    evens, odds = [swap_even(piece, count) for piece in part], [None, None]
    evens[0], proj, total, *parts = tie(
        evens[0], proj, total, *parts
    )
    parts += project(plan, places["chunks"] + 1, len(chunks) - 1, proj, in_weight, deep)
    for phase in range(2, count):
        for_even[phase], parts = parts[:2], parts[2:]
        if 2 * phase <= count:
            for_odd[phase + 1] = for_even[phase]
        elif phase + 1 < count:
            for_odd[phase + 1], parts = parts[:2], parts[2:]
    for phase in range(2, count):
        if phase > 2:
            for piece in range(2):
                evens[piece], odds[piece] = tie(evens[piece], odds[piece])
        if phase == count - 1:
            odds[0], total = tie(odds[0], total)
        for piece in range(2):
            next_even = swap_even(added(for_even[phase][piece], masked(odds[piece])), count)
            odds[piece] = swap_odd(added(for_odd[phase][piece], evens[piece]), count, blocks)
            evens[piece] = next_even
    mask = 1
    while 2 * mask < blocks:
        total = total + swap_ctx(total, mask, blocks)
        mask *= 2
    other = swap_ctx(total, mask, blocks)
    evens[0], odds[0], evens[1], other = tie(evens[0], odds[0], evens[1], other)
    grad_residue = (total + other) / (tokens * blocks)
    grad_input = jnp.concatenate(
        [added(parts[piece], evens[piece], masked(odds[piece])) for piece in range(2)]
    )
    return grad_input, grad_residue


def solution(mesh):
    return jax.shard_map(
        local,
        mesh=mesh,
        in_specs=(
            P(None, "ctx", "chan"),
            P("ctx", "chan"),
            P("ctx", "chan"),
            P("chan", None),
            P(None, None, "chan"),
            P(None, None, "chan"),
            P(None, "chan"),
            P(None, "chan"),
        ),
        out_specs=(P("chan", "ctx"), P(None, "chan")),
        check_vma=False,
    )
```

```python
import functools

import jax
import jax.numpy as jnp
from jax import lax
from jax.experimental import pallas as pl
from jax.experimental.pallas import tpu as pltpu
from jax.sharding import PartitionSpec as P

LANES = 128
ROWS = 8
NT = (((1,), (1,)), ((), ()))
VMEM = pl.BlockSpec(memory_space=pltpu.VMEM)
HBM = pl.BlockSpec(memory_space=pltpu.HBM)
SMEM = pl.BlockSpec(memory_space=pltpu.SMEM)
GRANT = 46 * 2**20
TAIL = 16
SMALL = pl.CostEstimate(flops=1, bytes_accessed=1, transcendentals=0)


def tile(token):
    return pl.ds(pl.multiple_of(token * ROWS, ROWS), ROWS)


def tree_sum(terms):
    terms = list(terms)
    while len(terms) > 1:
        paired = [a + b for a, b in zip(terms[::2], terms[1::2])]
        terms = paired + terms[2 * len(paired):]
    return terms[0]


def spread_kernel(features, saved, *outs):
    tokens, width = saved.shape
    if width < ROWS * LANES:
        for out in outs:
            out[...] = jnp.zeros(out.shape, out.dtype)
    for group in range(width // LANES):
        columns = pl.ds(group * LANES, LANES)
        rows = pl.ds(group, tokens, stride=ROWS)
        for which in range(3):
            outs[which][rows, :] = features[which, :, columns].astype(jnp.float32)
        outs[3][rows, :] = saved[:, columns].astype(jnp.float32)
        outs[4][rows, :] = (
            features[1, :, columns].astype(jnp.float32) * features[2, :, columns].astype(jnp.float32)
        )


def spread_acts(features, saved):
    flat = jax.ShapeDtypeStruct((saved.shape[0] * ROWS, LANES), jnp.float32)
    return pl.pallas_call(
        spread_kernel,
        in_specs=[VMEM] * 2,
        out_specs=[VMEM] * 5,
        out_shape=[flat] * 5,
        compiler_params=pltpu.CompilerParams(vmem_limit_bytes=GRANT),
        cost_estimate=SMALL,
        name="spread",
    )(features, saved)


def gate_kernel(at, has_acc, shards, count, halves, plan, *refs):
    acc = refs[0] if has_acc else None
    pieces = [
        jnp.concatenate([refs[has_acc + halves * i + part][...] for part in range(halves)])
        for i in range(count)
    ]
    weight, out, buffer, sems = refs[has_acc + halves * count:]
    width, deep = buffer.shape[1:]
    block = min(256, width)
    copies = []
    for shard in range(shards):
        columns = pl.ds(pl.multiple_of(plan[at + shard] * deep, deep), deep)
        copies.append(
            pltpu.make_async_copy(weight.at[:, columns], buffer.at[shard], sems.at[shard])
        )
        copies[-1].start()
    if shards < count:
        pieces = [jnp.where(plan[at + 1] > 0, *pieces)]
    elif shards > 1:
        pieces = [
            jnp.where(plan[at + shards + i] > 0, piece, jnp.zeros_like(piece))
            for i, piece in enumerate(pieces)
        ]
    for shard in range(shards):
        copies[shard].wait()
        for start in range(0, width, block):
            rows = pl.ds(start, block)
            value = lax.dot_general(
                pieces[shard], buffer[shard, rows, :], NT, preferred_element_type=jnp.float32
            )
            if shard:
                value = value + out[:, rows]
            elif has_acc:
                value = value + acc[:, rows]
            out[:, rows] = value


def gate_step(plan, at, acc, pieces, weight, shards):
    halves = len(pieces[0])
    tokens, deep = halves * pieces[0][0].shape[0], pieces[0][0].shape[1]
    width = weight.shape[0]
    has_acc = acc is not None
    flat = [piece for shard in pieces for piece in shard]
    return pl.pallas_call(
        functools.partial(gate_kernel, at, has_acc, shards, len(pieces), halves),
        in_specs=[SMEM] + [VMEM] * (has_acc + len(flat)) + [HBM],
        out_specs=VMEM,
        out_shape=jax.ShapeDtypeStruct((tokens, width), jnp.float32),
        scratch_shapes=[
            pltpu.VMEM((shards, width, deep), jnp.bfloat16),
            pltpu.SemaphoreType.DMA((shards,)),
        ],
        compiler_params=pltpu.CompilerParams(vmem_limit_bytes=GRANT),
        cost_estimate=SMALL,
        name="gate_step",
    )(plan, *([acc] if has_acc else []), *flat, weight)


def close_kernel(at, extra, late, plan, acc, piece, weight, query, saved, lam, other, *refs):
    if late:
        residues, (gconv, gquery, packet, products, gate) = other, refs
    else:
        later, (gconv, gquery, packet, gate) = other, refs
    tokens = piece.shape[0]
    first = tokens if late else 0
    width = weight.shape[0]
    poles = lam.shape[0]
    block = min(256, width)
    if width < ROWS * LANES:
        gate[...] = jnp.zeros(gate.shape, gate.dtype)
    arrived = jnp.where(plan[at] > 0, piece[...], jnp.zeros(piece.shape, piece.dtype))
    for start in range(0, width, block):
        columns = pl.ds(start, block)
        value = acc[pl.ds(first, tokens), columns] + lax.dot_general(
            arrived, weight[columns, :], NT, preferred_element_type=jnp.float32
        )
        for group in range(block // LANES):
            rows = pl.ds(start // LANES + group, tokens, stride=ROWS)
            gate[rows, :] = value[:, group * LANES:(group + 1) * LANES]

    def body(n, state):
        token = tokens - 1 - n
        here = tile(token)
        there = tile(first + token)
        grad = gate[here, :]
        conv = grad * query[there, :]
        gconv[here, :] = conv
        gquery[here, :] = grad * saved[there, :]
        state = tuple(lam[m] * state[m] + conv for m in range(poles))
        if late:
            products[here, :] = tree_sum([residues[m] * state[m] for m in range(poles)])
        return state

    if late:
        state = (jnp.zeros((ROWS, LANES), jnp.float32),) * poles
    else:
        state = tuple(later[m] for m in range(poles))
    state = lax.fori_loop(0, tokens, body, state, unroll=8)
    for m in range(poles):
        packet[m] = state[m]
    if not late:
        for row in range(extra - 1):
            packet[poles + row] = gconv[tile(row), :]
        for row in range(extra):
            packet[poles + extra - 1 + row] = gquery[tile(row), :]


def close_gate(plan, at, acc, piece, weight, query, saved, lam, extra, residues=None, later=None):
    tokens, deep = piece.shape
    width = weight.shape[0]
    poles = lam.shape[0]
    late = later is None
    flat = jax.ShapeDtypeStruct((tokens * ROWS, LANES), jnp.float32)
    packed = (poles if late else poles + 2 * extra - 1, ROWS, LANES)
    outs = [flat, flat, jax.ShapeDtypeStruct(packed, jnp.float32)] + [flat] * late
    return pl.pallas_call(
        functools.partial(close_kernel, at, extra, late),
        in_specs=[SMEM] + [VMEM] * 7,
        out_specs=[VMEM] * len(outs),
        out_shape=outs,
        scratch_shapes=[pltpu.VMEM(flat.shape, jnp.float32)],
        compiler_params=pltpu.CompilerParams(vmem_limit_bytes=GRANT),
        cost_estimate=SMALL,
        name="close_gate",
    )(plan, acc, piece, weight, query, saved, lam, residues if late else later)


def fold_kernel(plan, own, other, span, chip):
    poles = span.shape[0]
    first = plan[0] % 2 == 0
    for row in range(own.shape[0]):
        value = jnp.where(first, own[row], other[row])
        if row < poles:
            value = value + span[row] * jnp.where(first, other[row], own[row])
        chip[row] = value.astype(chip.dtype)


def fold(plan, own, other, span):
    return pl.pallas_call(
        fold_kernel,
        in_specs=[SMEM] + [VMEM] * 3,
        out_specs=VMEM,
        out_shape=jax.ShapeDtypeStruct(own.shape, jnp.float32),
        compiler_params=pltpu.CompilerParams(vmem_limit_bytes=GRANT),
        cost_estimate=SMALL,
        name="fold",
    )(plan, own, other, span)


def filtered(filters, which, now, later):
    return tree_sum(
        [filters[which, 0] * now]
        + [filters[which, lag + 1] * value for lag, value in enumerate(later)]
    )


def gather_rows(spread, out, first, tokens):
    for group in range(out.shape[-1] // LANES):
        out[pl.ds(first, tokens), pl.ds(group * LANES, LANES)] = spread[
            pl.ds(first * ROWS + group, tokens, stride=ROWS), :
        ].astype(out.dtype)


def settle_kernel(
    taps, later, late_conv, late_query, early_conv, early_query, lam, residues, filters,
    products, passed, queries, spread,
):
    extra = taps - 1
    half = late_conv.shape[0] // ROWS
    poles = lam.shape[0]

    def late_body(n, after):
        token = half - TAIL - 1 - n
        now = late_query[tile(token), :]
        spread[tile(half + token), :] = filtered(filters, 0, now, after)
        return (now,) + after[:-1]

    after = tuple(late_query[tile(half - TAIL + row), :] for row in range(extra))
    after = lax.fori_loop(0, half - TAIL, late_body, after, unroll=8)

    def body(n, carry):
        state, after = carry
        here = tile(half - 1 - n)
        conv = early_conv[here, :]
        passed[here, :] = conv
        passed[tile(2 * half - 1 - n), :] = late_conv[here, :]
        state = tuple(lam[m] * state[m] + conv for m in range(poles))
        products[here, :] = tree_sum([residues[m] * state[m] for m in range(poles)])
        now = early_query[here, :]
        spread[here, :] = filtered(filters, 0, now, after)
        return state, (now,) + after[:-1]

    state = tuple(later[m] for m in range(poles))
    lax.fori_loop(0, half, body, (state, after), unroll=8)
    gather_rows(spread, queries, 0, 2 * half - TAIL)


def settle(later, late_conv, late_query, early_conv, early_query, lam, residues, filters, width):
    taps = filters.shape[1]
    half = late_conv.shape[0] // ROWS
    return pl.pallas_call(
        functools.partial(settle_kernel, taps),
        in_specs=[VMEM] * 8,
        out_specs=[VMEM] * 3,
        out_shape=[
            jax.ShapeDtypeStruct(early_conv.shape, jnp.float32),
            jax.ShapeDtypeStruct((2 * half * ROWS, LANES), jnp.float32),
            jax.ShapeDtypeStruct((2 * half, width), jnp.bfloat16),
        ],
        scratch_shapes=[pltpu.VMEM((2 * half * ROWS, LANES), jnp.float32)],
        compiler_params=pltpu.CompilerParams(vmem_limit_bytes=GRANT),
        cost_estimate=SMALL,
        name="settle",
    )(later, late_conv, late_query, early_conv, early_query, lam, residues, filters)


def scan_kernel(
    at_plan, taps, chips, plan, late_products, early_products, queries, late_query, key_acts,
    value_acts, lam, rate, residues, filters, kv_halo, own, other, *refs,
):
    arrived = refs[:chips - 1]
    weight, proj, chunk, chunk_rest, entering, spread, buffer, sem = refs[chips - 1:]
    extra = taps - 1
    tokens, width = proj.shape[1:]
    half = tokens // 2
    poles = lam.shape[0]
    rows = 2 * chunk.shape[0]
    copy = pltpu.make_async_copy(
        weight.at[:, pl.ds(pl.multiple_of(plan[at_plan] * rows, rows), rows), :], buffer, sem
    )
    copy.start()

    block = plan[0]
    core, here = block % 2, block // 2
    for m in range(poles):
        beyond = []
        for mask in range(1, chips):
            there = here ^ mask
            distance = (2 * tokens * jnp.maximum(there - here - 1, 0)).astype(jnp.float32)
            term = jnp.exp(-rate[m] * distance) * arrived[mask - 1][m].astype(jnp.float32)
            beyond.append(jnp.where(there > here, term, jnp.zeros_like(term)))
        beyond = tree_sum(beyond)
        entering[m] = jnp.where(
            core == 0, other[m] + jnp.exp(-rate[m] * tokens) * beyond, beyond
        )
    halo = []
    for row in range(poles, poles + 2 * extra - 1):
        value = jnp.where(core == 0, other[row], jnp.zeros_like(other[row]))
        for mask in range(1, chips):
            there = here ^ mask
            value = jnp.where(
                (core == 1) & (there == here + 1), arrived[mask - 1][row].astype(jnp.float32), value
            )
        halo.append(value)

    state = [entering[m] for m in range(poles)]
    parts = tuple(residues[m] * state[m] for m in range(poles))
    keys, values, after = [], [], []
    for row in range(extra):
        if row:
            state = [(state[m] - halo[row - 1]) * jnp.exp(rate[m]) for m in range(poles)]
        product = tree_sum([residues[m] * state[m] for m in range(poles)])
        keys.append(product * kv_halo[1, row])
        values.append(product * kv_halo[0, row])
        after.append(halo[extra - 1 + row])

    for token in range(tokens - 1, tokens - TAIL - 1, -1):
        now = late_query[pl.ds((token - half) * ROWS, ROWS), :]
        spread[0, pl.ds(token * ROWS, ROWS), :] = filtered(filters, 0, now, after)
        after = [now] + after[:-1]
    proj[0, pl.ds(0, tokens - TAIL), :] = queries[pl.ds(0, tokens - TAIL), :]
    gather_rows(spread.at[0], proj.at[0], tokens - TAIL, TAIL)

    def body(first, products, n, carry):
        parts, later = carry
        token = half - 1 - n
        at = tile(first + token)
        parts = tuple(lam[m] * parts[m] for m in range(poles))
        product = products[tile(token), :] + tree_sum(parts)
        now = (product * value_acts[at, :], product * key_acts[at, :])
        for which in range(2):
            spread[1 + which, at, :] = filtered(filters, 1 + which, now[which], later[which])
        return parts, tuple((now[which],) + later[which][:-1] for which in range(2))

    carry = (parts, (tuple(keys), tuple(values)))
    for first, products in ((half, late_products), (0, early_products)):
        carry = lax.fori_loop(0, half, functools.partial(body, first, products), carry, unroll=8)
    for which in range(1, 3):
        gather_rows(spread.at[which], proj.at[which], 0, tokens)
    copy.wait()
    project_rows(buffer, proj, (chunk, chunk_rest))


def scan_block(plan, at, settled, keys, values, lam, rate, residues, filters, kv_halo, own, other,
               arrived, weight, deep, width):
    tokens = keys.shape[0] // ROWS
    taps = filters.shape[1]
    return pl.pallas_call(
        functools.partial(scan_kernel, at, taps, len(arrived) + 1),
        in_specs=[SMEM] + [VMEM] * (13 + len(arrived)) + [HBM],
        out_specs=[VMEM] * 4,
        out_shape=[
            jax.ShapeDtypeStruct((3, tokens, width), jnp.bfloat16),
            jax.ShapeDtypeStruct((deep // 2, tokens), jnp.bfloat16),
            jax.ShapeDtypeStruct((deep // 2, tokens), jnp.bfloat16),
            jax.ShapeDtypeStruct(lam.shape, jnp.float32),
        ],
        scratch_shapes=[
            pltpu.VMEM((3, tokens * ROWS, LANES), jnp.float32),
            pltpu.VMEM((3, deep, width), jnp.bfloat16),
            pltpu.SemaphoreType.DMA,
        ],
        compiler_params=pltpu.CompilerParams(vmem_limit_bytes=GRANT),
        cost_estimate=SMALL,
        name="scan",
    )(plan, *settled, keys, values, lam, rate, residues, filters, kv_halo, own, other, *arrived, weight)


def project_rows(weight, proj, outs):
    rows = outs[0].shape[0]
    block = min(256, rows)
    for part, out in enumerate(outs):
        for start in range(0, rows, block):
            value = tree_sum([
                lax.dot_general(
                    weight[which, pl.ds(part * rows + start, block), :], proj[which],
                    NT, preferred_element_type=jnp.float32,
                )
                for which in range(3)
            ])
            out[pl.ds(start, block), :] = value.astype(out.dtype)


def add_up_residues(tiles_of, gconv, product, lam, entering, total):
    tokens = gconv.shape[0] // ROWS
    poles = lam.shape[0]

    def body(n, carry):
        state, sums = carry
        at = tile(tokens - 1 - n)
        conv, both = gconv[at, :], product[at, :]
        state = tuple(lam[m] * state[m] + conv for m in range(poles))
        return state, tuple(sums[m] + both * state[m] for m in range(poles))

    state = tuple(entering[m] for m in range(poles))
    zero = jnp.zeros((ROWS, LANES), jnp.float32)
    _, sums = lax.fori_loop(0, tokens, body, (state, (zero,) * poles), unroll=8)
    for m in range(poles):
        tiles_of[pl.ds(m * ROWS, ROWS), :] = sums[m]
    gather_rows(tiles_of, total, 0, poles)


def project_kernel(at, count, sources, plan, proj, weight, *refs):
    if sources:
        add_up = functools.partial(add_up_residues, refs[-1], *refs[:sources + 1])
        refs = refs[sources + 1:-1]
    outs, (buffer, sems) = refs[:2 * count], refs[2 * count:]
    deep = buffer.shape[2]
    copies = []
    for i in range(count):
        start = pl.multiple_of(plan[at + i] * deep, deep)
        copies.append(
            pltpu.make_async_copy(weight.at[:, pl.ds(start, deep), :], buffer.at[i], sems.at[i])
        )
        copies[-1].start()
    if sources:
        add_up()
    for i in range(count):
        copies[i].wait()
        project_rows(buffer.at[i], proj, outs[2 * i:2 * i + 2])


def project(plan, at, count, proj, weight, deep, sources=()):
    _, tokens, width = proj.shape
    outs = [jax.ShapeDtypeStruct((deep // 2, tokens), jnp.bfloat16)] * (2 * count)
    if sources:
        outs = [jax.ShapeDtypeStruct((sources[-1].shape[0], width), jnp.float32)] + outs
    return pl.pallas_call(
        functools.partial(project_kernel, at, count, len(sources)),
        in_specs=[SMEM, VMEM, HBM] + [VMEM] * len(sources),
        out_specs=[VMEM] * len(outs),
        out_shape=outs,
        scratch_shapes=[
            pltpu.VMEM((count, 3, deep, width), jnp.bfloat16),
            pltpu.SemaphoreType.DMA((count,)),
        ] + [pltpu.VMEM((array.shape[0] * ROWS, LANES), jnp.float32) for array in sources[-1:]],
        compiler_params=pltpu.CompilerParams(vmem_limit_bytes=GRANT),
        cost_estimate=pl.CostEstimate(
            flops=6 * tokens * width * deep * count,
            bytes_accessed=6 * width * deep * count,
            transcendentals=0,
        ),
        name="project",
    )(plan, proj, weight, *sources)


def scalars(*values):
    return jnp.stack([jnp.asarray(value, jnp.int32) for value in values])


def tiles(array):
    lead = array.shape[:-1]
    groups = array.shape[-1] // LANES
    array = array.reshape(lead + (groups, LANES))
    if groups < ROWS:
        array = jnp.pad(array, [(0, 0)] * len(lead) + [(0, ROWS - groups), (0, 0)])
    return array


def swap_even(value, count):
    return lax.ppermute(value, "chan", [(i, i ^ 1) for i in range(count)])


def swap_odd(value, count, blocks):
    pairs = []
    for block in range(blocks):
        for i in range(count):
            other = i + 1 if i % 2 else i - 1
            if 0 <= other < count:
                pairs.append((block * count + i, block * count + other))
            else:
                pairs.append((block * count + i, (block ^ 1) * count + i))
    return lax.ppermute(value, ("ctx", "chan"), pairs)


def swap_ctx(value, mask, blocks):
    return lax.ppermute(value, "ctx", [(i, i ^ mask) for i in range(blocks)])


def tie(*values):
    return lax.optimization_barrier(values)


def local(features, saved_conv, grad_out, out_weight, in_weight, short_taps, residues, decay_time):
    f32, bf16 = jnp.float32, jnp.bfloat16
    tokens, width = saved_conv.shape
    taps = short_taps.shape[1]
    extra = taps - 1
    poles = residues.shape[0]
    count = lax.axis_size("chan")
    me = lax.axis_index("chan")
    even = me % 2 == 0
    deep = in_weight.shape[1] // count
    blocks = lax.axis_size("ctx")
    block = lax.axis_index("ctx")

    rate = tiles(1.0 / decay_time)
    lam = jnp.exp(-rate)
    span = jnp.exp(-rate * tokens)
    res = tiles(residues)
    filters = tiles(short_taps)

    def shared(phase):
        far = count - phase
        as_even = jnp.where(me < phase, me + far, jnp.maximum(me - far + 1, 0))
        as_odd = jnp.where(me >= far, me - far, jnp.minimum(me + far - 1, count - 1))
        return jnp.where(even, as_even, as_odd)

    def reached(phase, along):
        right = jnp.minimum(me + count - phase, count - 1)
        left = jnp.maximum(me - (count - phase), 0)
        return jnp.where(along, right, left)

    def shards(phase):
        above, below = me + phase, me - phase
        high, low = jnp.minimum(above, count - 1), jnp.maximum(below, 0)
        at_even, at_odd = jnp.where(even, high, low), jnp.where(even, low, high)
        even_ok = jnp.where(even, above < count, below >= 0)
        odd_ok = jnp.where(even, below >= 0, above < count)
        if 2 * phase == count:
            return [jnp.where(even_ok, at_even, at_odd), even_ok]
        return [at_even, at_odd, even_ok, odd_ok]

    edge = (me == 0) | (me == count - 1)
    plan, places = [block, edge], {}

    def planned(name, values):
        places[name] = len(plan)
        plan.extend(values)

    planned("own", [me, 1])
    for phase in range(1, count - 1):
        planned(("gate", phase), shards(phase))
    planned("first", [shared(1)])
    chunks = []
    for phase in range(2, count):
        if 2 * phase <= count:
            chunks.append(shared(phase))
        else:
            chunks.append(reached(phase, even))
            if phase + 1 < count:
                chunks.append(reached(phase + 1, ~even))
    chunks.append(me)
    planned("chunks", chunks)
    plan = scalars(*plan)

    half = tokens // 2
    evens = [swap_even(grad_out[half:], count)]
    odds = [swap_odd(grad_out[half:], count, blocks)]
    rest, plan, rate, lam, span, res, filters = tie(grad_out, plan, rate, lam, span, res, filters)
    evens.append(swap_even(rest[:half], count))
    odds.append(swap_odd(rest[:half], count, blocks))
    evens[0], odds[0] = tie(evens[0], odds[0])
    acc = None
    for phase in range(1, count - 1):
        ahead = [[swap_even(odds[0], count)], [swap_odd(evens[0], count, blocks)]]
        if phase == 1:
            acc = gate_step(plan, places["own"], None, [[grad_out]], out_weight, 1)
            evens[1], odds[1], acc = tie(evens[1], odds[1], acc)
        ahead[0].append(swap_even(odds[1], count))
        ahead[1].append(swap_odd(evens[1], count, blocks))
        acc = gate_step(
            plan, places["gate", phase], acc, [evens[::-1], odds[::-1]], out_weight,
            1 if 2 * phase == count else 2,
        )
        evens, odds = ahead
        if phase < count - 2:
            evens[0], odds[0], acc = tie(evens[0], odds[0], acc)
            evens[1], odds[1] = tie(evens[1], odds[1])
        if phase == 1:
            odds[0], features, saved_conv = tie(odds[0], features, saved_conv)
            kv_halo = tiles(features[1:3, :extra].astype(f32))
            kv_halo = lax.ppermute(kv_halo, "ctx", [(i, (i - 1) % blocks) for i in range(blocks)])
            last = jnp.where(
                even, jnp.minimum(count - 1, me + count - 1), jnp.maximum(me - count + 1, 0)
            )
            last_weight = lax.dynamic_slice(out_weight, (0, last * width), (width, width))
            query, keys, values, saved, product = spread_acts(features, saved_conv)
            odds[1], kv_halo, last_weight = tie(odds[1], kv_halo, last_weight)
    late_conv, late_query, later, late_products = close_gate(
        plan, 1, acc, evens[0], last_weight, query, saved, lam, extra, residues=res
    )
    early_conv, early_query, packet = close_gate(
        plan, 1, acc, evens[1], last_weight, query, saved, lam, extra, later=later
    )

    other = swap_ctx(packet, 1, blocks)
    chip = fold(plan, packet, other, span)
    arrived = [swap_ctx(chip, 2 * mask, blocks) for mask in range(1, blocks // 2)]
    early_products, gconv, queries = settle(
        later, late_conv, late_query, early_conv, early_query, lam, res, filters, width
    )

    def added(*parts):
        return sum(value.astype(f32) for value in parts if value is not None).astype(bf16)

    def masked(value):
        return None if value is None else jnp.where(edge, jnp.zeros_like(value), value)

    proj, *part, entering = scan_block(
        plan, places["first"], [late_products, early_products, queries, late_query], keys, values,
        lam, rate, res, filters, kv_halo, packet, other, arrived, in_weight, deep, width,
    )
    total, *parts = project(
        plan, places["chunks"], 1, proj, in_weight, deep, [gconv, product, lam, entering]
    )
    for_even, for_odd = {1: part}, {2: part}
    evens, odds = [swap_even(piece, count) for piece in part], [None, None]
    evens[0], proj, total, *parts = tie(
        evens[0], proj, total, *parts
    )
    parts += project(plan, places["chunks"] + 1, len(chunks) - 1, proj, in_weight, deep)
    for phase in range(2, count):
        for_even[phase], parts = parts[:2], parts[2:]
        if 2 * phase <= count:
            for_odd[phase + 1] = for_even[phase]
        elif phase + 1 < count:
            for_odd[phase + 1], parts = parts[:2], parts[2:]
    for phase in range(2, count):
        if phase > 2:
            for piece in range(2):
                evens[piece], odds[piece] = tie(evens[piece], odds[piece])
        if phase == count - 1:
            odds[0], total = tie(odds[0], total)
        for piece in range(2):
            next_even = swap_even(added(for_even[phase][piece], masked(odds[piece])), count)
            odds[piece] = swap_odd(added(for_odd[phase][piece], evens[piece]), count, blocks)
            evens[piece] = next_even
    mask = 1
    while 2 * mask < blocks:
        total = total + swap_ctx(total, mask, blocks)
        mask *= 2
    other = swap_ctx(total, mask, blocks)
    evens[0], odds[0], evens[1], other = tie(evens[0], odds[0], evens[1], other)
    grad_residue = (total + other) / (tokens * blocks)
    grad_input = jnp.concatenate(
        [added(parts[piece], evens[piece], masked(odds[piece])) for piece in range(2)]
    )
    return grad_input, grad_residue


def solution(mesh):
    return jax.shard_map(
        local,
        mesh=mesh,
        in_specs=(
            P(None, "ctx", "chan"),
            P("ctx", "chan"),
            P("ctx", "chan"),
            P("chan", None),
            P(None, None, "chan"),
            P(None, None, "chan"),
            P(None, "chan"),
            P(None, "chan"),
        ),
        out_specs=(P("chan", "ctx"), P(None, "chan")),
        check_vma=False,
    )
```

```python
import functools

import jax
import jax.numpy as jnp
from jax import lax
from jax.experimental import pallas as pl
from jax.experimental.pallas import tpu as pltpu
from jax.sharding import PartitionSpec as P

LANES = 128
ROWS = 8
NT = (((1,), (1,)), ((), ()))
VMEM = pl.BlockSpec(memory_space=pltpu.VMEM)
HBM = pl.BlockSpec(memory_space=pltpu.HBM)
SMEM = pl.BlockSpec(memory_space=pltpu.SMEM)
GRANT = 46 * 2**20
TAIL = 16
SMALL = pl.CostEstimate(flops=1, bytes_accessed=1, transcendentals=0)


def tile(token):
    return pl.ds(pl.multiple_of(token * ROWS, ROWS), ROWS)


def tree_sum(terms):
    terms = list(terms)
    while len(terms) > 1:
        paired = [a + b for a, b in zip(terms[::2], terms[1::2])]
        terms = paired + terms[2 * len(paired):]
    return terms[0]


def spread_kernel(features, saved, *outs):
    tokens, width = saved.shape
    if width < ROWS * LANES:
        for out in outs:
            out[...] = jnp.zeros(out.shape, out.dtype)
    for group in range(width // LANES):
        columns = pl.ds(group * LANES, LANES)
        rows = pl.ds(group, tokens, stride=ROWS)
        for which in range(3):
            outs[which][rows, :] = features[which, :, columns].astype(jnp.float32)
        outs[3][rows, :] = saved[:, columns].astype(jnp.float32)
        outs[4][rows, :] = (
            features[1, :, columns].astype(jnp.float32) * features[2, :, columns].astype(jnp.float32)
        )


def spread_acts(features, saved):
    flat = jax.ShapeDtypeStruct((saved.shape[0] * ROWS, LANES), jnp.float32)
    return pl.pallas_call(
        spread_kernel,
        in_specs=[VMEM] * 2,
        out_specs=[VMEM] * 5,
        out_shape=[flat] * 5,
        compiler_params=pltpu.CompilerParams(vmem_limit_bytes=GRANT),
        cost_estimate=SMALL,
        name="spread",
    )(features, saved)


def gate_kernel(at, has_acc, shards, count, halves, plan, *refs):
    acc = refs[0] if has_acc else None
    pieces = [
        jnp.concatenate([refs[has_acc + halves * i + part][...] for part in range(halves)])
        for i in range(count)
    ]
    weight, out, buffer, sems = refs[has_acc + halves * count:]
    width, deep = buffer.shape[1:]
    block = min(256, width)
    copies = []
    for shard in range(shards):
        columns = pl.ds(pl.multiple_of(plan[at + shard] * deep, deep), deep)
        copies.append(
            pltpu.make_async_copy(weight.at[:, columns], buffer.at[shard], sems.at[shard])
        )
        copies[-1].start()
    if shards < count:
        pieces = [jnp.where(plan[at + 1] > 0, *pieces)]
    elif shards > 1:
        pieces = [
            jnp.where(plan[at + shards + i] > 0, piece, jnp.zeros_like(piece))
            for i, piece in enumerate(pieces)
        ]
    for shard in range(shards):
        copies[shard].wait()
        for start in range(0, width, block):
            rows = pl.ds(start, block)
            value = lax.dot_general(
                pieces[shard], buffer[shard, rows, :], NT, preferred_element_type=jnp.float32
            )
            if shard:
                value = value + out[:, rows]
            elif has_acc:
                value = value + acc[:, rows]
            out[:, rows] = value


def gate_step(plan, at, acc, pieces, weight, shards):
    halves = len(pieces[0])
    tokens, deep = halves * pieces[0][0].shape[0], pieces[0][0].shape[1]
    width = weight.shape[0]
    has_acc = acc is not None
    flat = [piece for shard in pieces for piece in shard]
    return pl.pallas_call(
        functools.partial(gate_kernel, at, has_acc, shards, len(pieces), halves),
        in_specs=[SMEM] + [VMEM] * (has_acc + len(flat)) + [HBM],
        out_specs=VMEM,
        out_shape=jax.ShapeDtypeStruct((tokens, width), jnp.float32),
        scratch_shapes=[
            pltpu.VMEM((shards, width, deep), jnp.bfloat16),
            pltpu.SemaphoreType.DMA((shards,)),
        ],
        compiler_params=pltpu.CompilerParams(vmem_limit_bytes=GRANT),
        cost_estimate=SMALL,
        name="gate_step",
    )(plan, *([acc] if has_acc else []), *flat, weight)


def close_kernel(at, extra, late, plan, acc, piece, weight, query, saved, lam, other, *refs):
    if late:
        residues, (gconv, gquery, packet, products, gate) = other, refs
    else:
        later, (gconv, gquery, packet, gate) = other, refs
    tokens = piece.shape[0]
    first = tokens if late else 0
    width = weight.shape[0]
    poles = lam.shape[0]
    block = min(256, width)
    if width < ROWS * LANES:
        gate[...] = jnp.zeros(gate.shape, gate.dtype)
    arrived = jnp.where(plan[at] > 0, piece[...], jnp.zeros(piece.shape, piece.dtype))
    for start in range(0, width, block):
        columns = pl.ds(start, block)
        value = acc[pl.ds(first, tokens), columns] + lax.dot_general(
            arrived, weight[columns, :], NT, preferred_element_type=jnp.float32
        )
        for group in range(block // LANES):
            rows = pl.ds(start // LANES + group, tokens, stride=ROWS)
            gate[rows, :] = value[:, group * LANES:(group + 1) * LANES]

    def body(n, state):
        token = tokens - 1 - n
        here = tile(token)
        there = tile(first + token)
        grad = gate[here, :]
        conv = grad * query[there, :]
        gconv[here, :] = conv
        gquery[here, :] = grad * saved[there, :]
        state = tuple(lam[m] * state[m] + conv for m in range(poles))
        if late:
            products[here, :] = tree_sum([residues[m] * state[m] for m in range(poles)])
        return state

    if late:
        state = (jnp.zeros((ROWS, LANES), jnp.float32),) * poles
    else:
        state = tuple(later[m] for m in range(poles))
    state = lax.fori_loop(0, tokens, body, state, unroll=16)
    for m in range(poles):
        packet[m] = state[m]
    if not late:
        for row in range(extra - 1):
            packet[poles + row] = gconv[tile(row), :]
        for row in range(extra):
            packet[poles + extra - 1 + row] = gquery[tile(row), :]


def close_gate(plan, at, acc, piece, weight, query, saved, lam, extra, residues=None, later=None):
    tokens, deep = piece.shape
    width = weight.shape[0]
    poles = lam.shape[0]
    late = later is None
    flat = jax.ShapeDtypeStruct((tokens * ROWS, LANES), jnp.float32)
    packed = (poles if late else poles + 2 * extra - 1, ROWS, LANES)
    outs = [flat, flat, jax.ShapeDtypeStruct(packed, jnp.float32)] + [flat] * late
    return pl.pallas_call(
        functools.partial(close_kernel, at, extra, late),
        in_specs=[SMEM] + [VMEM] * 7,
        out_specs=[VMEM] * len(outs),
        out_shape=outs,
        scratch_shapes=[pltpu.VMEM(flat.shape, jnp.float32)],
        compiler_params=pltpu.CompilerParams(vmem_limit_bytes=GRANT),
        cost_estimate=SMALL,
        name="close_gate",
    )(plan, acc, piece, weight, query, saved, lam, residues if late else later)


def fold_kernel(plan, own, other, span, chip):
    poles = span.shape[0]
    first = plan[0] % 2 == 0
    for row in range(own.shape[0]):
        value = jnp.where(first, own[row], other[row])
        if row < poles:
            value = value + span[row] * jnp.where(first, other[row], own[row])
        chip[row] = value.astype(chip.dtype)


def fold(plan, own, other, span):
    return pl.pallas_call(
        fold_kernel,
        in_specs=[SMEM] + [VMEM] * 3,
        out_specs=VMEM,
        out_shape=jax.ShapeDtypeStruct(own.shape, jnp.float32),
        compiler_params=pltpu.CompilerParams(vmem_limit_bytes=GRANT),
        cost_estimate=SMALL,
        name="fold",
    )(plan, own, other, span)


def filtered(filters, which, now, later):
    return tree_sum(
        [filters[which, 0] * now]
        + [filters[which, lag + 1] * value for lag, value in enumerate(later)]
    )


def gather_rows(spread, out, first, tokens):
    for group in range(out.shape[-1] // LANES):
        out[pl.ds(first, tokens), pl.ds(group * LANES, LANES)] = spread[
            pl.ds(first * ROWS + group, tokens, stride=ROWS), :
        ].astype(out.dtype)


def settle_kernel(
    taps, later, late_conv, late_query, early_conv, early_query, lam, residues, filters,
    products, passed, queries, spread,
):
    extra = taps - 1
    half = late_conv.shape[0] // ROWS
    poles = lam.shape[0]

    def late_body(n, after):
        token = half - TAIL - 1 - n
        now = late_query[tile(token), :]
        spread[tile(half + token), :] = filtered(filters, 0, now, after)
        return (now,) + after[:-1]

    after = tuple(late_query[tile(half - TAIL + row), :] for row in range(extra))
    after = lax.fori_loop(0, half - TAIL, late_body, after, unroll=16)

    def body(n, carry):
        state, after = carry
        here = tile(half - 1 - n)
        conv = early_conv[here, :]
        passed[here, :] = conv
        passed[tile(2 * half - 1 - n), :] = late_conv[here, :]
        state = tuple(lam[m] * state[m] + conv for m in range(poles))
        products[here, :] = tree_sum([residues[m] * state[m] for m in range(poles)])
        now = early_query[here, :]
        spread[here, :] = filtered(filters, 0, now, after)
        return state, (now,) + after[:-1]

    state = tuple(later[m] for m in range(poles))
    lax.fori_loop(0, half, body, (state, after), unroll=16)
    gather_rows(spread, queries, 0, 2 * half - TAIL)


def settle(later, late_conv, late_query, early_conv, early_query, lam, residues, filters, width):
    taps = filters.shape[1]
    half = late_conv.shape[0] // ROWS
    return pl.pallas_call(
        functools.partial(settle_kernel, taps),
        in_specs=[VMEM] * 8,
        out_specs=[VMEM] * 3,
        out_shape=[
            jax.ShapeDtypeStruct(early_conv.shape, jnp.float32),
            jax.ShapeDtypeStruct((2 * half * ROWS, LANES), jnp.float32),
            jax.ShapeDtypeStruct((2 * half, width), jnp.bfloat16),
        ],
        scratch_shapes=[pltpu.VMEM((2 * half * ROWS, LANES), jnp.float32)],
        compiler_params=pltpu.CompilerParams(vmem_limit_bytes=GRANT),
        cost_estimate=SMALL,
        name="settle",
    )(later, late_conv, late_query, early_conv, early_query, lam, residues, filters)


def scan_kernel(
    at_plan, taps, chips, plan, late_products, early_products, queries, late_query, key_acts,
    value_acts, lam, rate, residues, filters, kv_halo, own, other, *refs,
):
    arrived = refs[:chips - 1]
    weight, proj, chunk, chunk_rest, entering, spread, buffer, sem = refs[chips - 1:]
    extra = taps - 1
    tokens, width = proj.shape[1:]
    half = tokens // 2
    poles = lam.shape[0]
    rows = 2 * chunk.shape[0]
    copy = pltpu.make_async_copy(
        weight.at[:, pl.ds(pl.multiple_of(plan[at_plan] * rows, rows), rows), :], buffer, sem
    )
    copy.start()

    block = plan[0]
    core, here = block % 2, block // 2
    for m in range(poles):
        beyond = []
        for mask in range(1, chips):
            there = here ^ mask
            distance = (2 * tokens * jnp.maximum(there - here - 1, 0)).astype(jnp.float32)
            term = jnp.exp(-rate[m] * distance) * arrived[mask - 1][m].astype(jnp.float32)
            beyond.append(jnp.where(there > here, term, jnp.zeros_like(term)))
        beyond = tree_sum(beyond)
        entering[m] = jnp.where(
            core == 0, other[m] + jnp.exp(-rate[m] * tokens) * beyond, beyond
        )
    halo = []
    for row in range(poles, poles + 2 * extra - 1):
        value = jnp.where(core == 0, other[row], jnp.zeros_like(other[row]))
        for mask in range(1, chips):
            there = here ^ mask
            value = jnp.where(
                (core == 1) & (there == here + 1), arrived[mask - 1][row].astype(jnp.float32), value
            )
        halo.append(value)

    state = [entering[m] for m in range(poles)]
    parts = tuple(residues[m] * state[m] for m in range(poles))
    keys, values, after = [], [], []
    for row in range(extra):
        if row:
            state = [(state[m] - halo[row - 1]) * jnp.exp(rate[m]) for m in range(poles)]
        product = tree_sum([residues[m] * state[m] for m in range(poles)])
        keys.append(product * kv_halo[1, row])
        values.append(product * kv_halo[0, row])
        after.append(halo[extra - 1 + row])

    for token in range(tokens - 1, tokens - TAIL - 1, -1):
        now = late_query[pl.ds((token - half) * ROWS, ROWS), :]
        spread[0, pl.ds(token * ROWS, ROWS), :] = filtered(filters, 0, now, after)
        after = [now] + after[:-1]
    proj[0, pl.ds(0, tokens - TAIL), :] = queries[pl.ds(0, tokens - TAIL), :]
    gather_rows(spread.at[0], proj.at[0], tokens - TAIL, TAIL)

    def body(first, products, n, carry):
        parts, later = carry
        token = half - 1 - n
        at = tile(first + token)
        parts = tuple(lam[m] * parts[m] for m in range(poles))
        product = products[tile(token), :] + tree_sum(parts)
        now = (product * value_acts[at, :], product * key_acts[at, :])
        for which in range(2):
            spread[1 + which, at, :] = filtered(filters, 1 + which, now[which], later[which])
        return parts, tuple((now[which],) + later[which][:-1] for which in range(2))

    carry = (parts, (tuple(keys), tuple(values)))
    for first, products in ((half, late_products), (0, early_products)):
        carry = lax.fori_loop(0, half, functools.partial(body, first, products), carry, unroll=16)
    for which in range(1, 3):
        gather_rows(spread.at[which], proj.at[which], 0, tokens)
    copy.wait()
    project_rows(buffer, proj, (chunk, chunk_rest))


def scan_block(plan, at, settled, keys, values, lam, rate, residues, filters, kv_halo, own, other,
               arrived, weight, deep, width):
    tokens = keys.shape[0] // ROWS
    taps = filters.shape[1]
    return pl.pallas_call(
        functools.partial(scan_kernel, at, taps, len(arrived) + 1),
        in_specs=[SMEM] + [VMEM] * (13 + len(arrived)) + [HBM],
        out_specs=[VMEM] * 4,
        out_shape=[
            jax.ShapeDtypeStruct((3, tokens, width), jnp.bfloat16),
            jax.ShapeDtypeStruct((deep // 2, tokens), jnp.bfloat16),
            jax.ShapeDtypeStruct((deep // 2, tokens), jnp.bfloat16),
            jax.ShapeDtypeStruct(lam.shape, jnp.float32),
        ],
        scratch_shapes=[
            pltpu.VMEM((3, tokens * ROWS, LANES), jnp.float32),
            pltpu.VMEM((3, deep, width), jnp.bfloat16),
            pltpu.SemaphoreType.DMA,
        ],
        compiler_params=pltpu.CompilerParams(vmem_limit_bytes=GRANT),
        cost_estimate=SMALL,
        name="scan",
    )(plan, *settled, keys, values, lam, rate, residues, filters, kv_halo, own, other, *arrived, weight)


def project_rows(weight, proj, outs):
    rows = outs[0].shape[0]
    block = min(256, rows)
    for part, out in enumerate(outs):
        for start in range(0, rows, block):
            value = tree_sum([
                lax.dot_general(
                    weight[which, pl.ds(part * rows + start, block), :], proj[which],
                    NT, preferred_element_type=jnp.float32,
                )
                for which in range(3)
            ])
            out[pl.ds(start, block), :] = value.astype(out.dtype)


def add_up_residues(tiles_of, gconv, product, lam, entering, total):
    tokens = gconv.shape[0] // ROWS
    poles = lam.shape[0]

    def body(n, carry):
        state, sums = carry
        at = tile(tokens - 1 - n)
        conv, both = gconv[at, :], product[at, :]
        state = tuple(lam[m] * state[m] + conv for m in range(poles))
        return state, tuple(sums[m] + both * state[m] for m in range(poles))

    state = tuple(entering[m] for m in range(poles))
    zero = jnp.zeros((ROWS, LANES), jnp.float32)
    _, sums = lax.fori_loop(0, tokens, body, (state, (zero,) * poles), unroll=16)
    for m in range(poles):
        tiles_of[pl.ds(m * ROWS, ROWS), :] = sums[m]
    gather_rows(tiles_of, total, 0, poles)


def project_kernel(at, count, sources, plan, proj, weight, *refs):
    if sources:
        add_up = functools.partial(add_up_residues, refs[-1], *refs[:sources + 1])
        refs = refs[sources + 1:-1]
    outs, (buffer, sems) = refs[:2 * count], refs[2 * count:]
    deep = buffer.shape[2]
    copies = []
    for i in range(count):
        start = pl.multiple_of(plan[at + i] * deep, deep)
        copies.append(
            pltpu.make_async_copy(weight.at[:, pl.ds(start, deep), :], buffer.at[i], sems.at[i])
        )
        copies[-1].start()
    if sources:
        add_up()
    for i in range(count):
        copies[i].wait()
        project_rows(buffer.at[i], proj, outs[2 * i:2 * i + 2])


def project(plan, at, count, proj, weight, deep, sources=()):
    _, tokens, width = proj.shape
    outs = [jax.ShapeDtypeStruct((deep // 2, tokens), jnp.bfloat16)] * (2 * count)
    if sources:
        outs = [jax.ShapeDtypeStruct((sources[-1].shape[0], width), jnp.float32)] + outs
    return pl.pallas_call(
        functools.partial(project_kernel, at, count, len(sources)),
        in_specs=[SMEM, VMEM, HBM] + [VMEM] * len(sources),
        out_specs=[VMEM] * len(outs),
        out_shape=outs,
        scratch_shapes=[
            pltpu.VMEM((count, 3, deep, width), jnp.bfloat16),
            pltpu.SemaphoreType.DMA((count,)),
        ] + [pltpu.VMEM((array.shape[0] * ROWS, LANES), jnp.float32) for array in sources[-1:]],
        compiler_params=pltpu.CompilerParams(vmem_limit_bytes=GRANT),
        cost_estimate=pl.CostEstimate(
            flops=6 * tokens * width * deep * count,
            bytes_accessed=6 * width * deep * count,
            transcendentals=0,
        ),
        name="project",
    )(plan, proj, weight, *sources)


def scalars(*values):
    return jnp.stack([jnp.asarray(value, jnp.int32) for value in values])


def tiles(array):
    lead = array.shape[:-1]
    groups = array.shape[-1] // LANES
    array = array.reshape(lead + (groups, LANES))
    if groups < ROWS:
        array = jnp.pad(array, [(0, 0)] * len(lead) + [(0, ROWS - groups), (0, 0)])
    return array


def swap_even(value, count):
    return lax.ppermute(value, "chan", [(i, i ^ 1) for i in range(count)])


def swap_odd(value, count, blocks):
    pairs = []
    for block in range(blocks):
        for i in range(count):
            other = i + 1 if i % 2 else i - 1
            if 0 <= other < count:
                pairs.append((block * count + i, block * count + other))
            else:
                pairs.append((block * count + i, (block ^ 1) * count + i))
    return lax.ppermute(value, ("ctx", "chan"), pairs)


def swap_ctx(value, mask, blocks):
    return lax.ppermute(value, "ctx", [(i, i ^ mask) for i in range(blocks)])


def tie(*values):
    return lax.optimization_barrier(values)


def local(features, saved_conv, grad_out, out_weight, in_weight, short_taps, residues, decay_time):
    f32, bf16 = jnp.float32, jnp.bfloat16
    tokens, width = saved_conv.shape
    taps = short_taps.shape[1]
    extra = taps - 1
    poles = residues.shape[0]
    count = lax.axis_size("chan")
    me = lax.axis_index("chan")
    even = me % 2 == 0
    deep = in_weight.shape[1] // count
    blocks = lax.axis_size("ctx")
    block = lax.axis_index("ctx")

    rate = tiles(1.0 / decay_time)
    lam = jnp.exp(-rate)
    span = jnp.exp(-rate * tokens)
    res = tiles(residues)
    filters = tiles(short_taps)

    def shared(phase):
        far = count - phase
        as_even = jnp.where(me < phase, me + far, jnp.maximum(me - far + 1, 0))
        as_odd = jnp.where(me >= far, me - far, jnp.minimum(me + far - 1, count - 1))
        return jnp.where(even, as_even, as_odd)

    def reached(phase, along):
        right = jnp.minimum(me + count - phase, count - 1)
        left = jnp.maximum(me - (count - phase), 0)
        return jnp.where(along, right, left)

    def shards(phase):
        above, below = me + phase, me - phase
        high, low = jnp.minimum(above, count - 1), jnp.maximum(below, 0)
        at_even, at_odd = jnp.where(even, high, low), jnp.where(even, low, high)
        even_ok = jnp.where(even, above < count, below >= 0)
        odd_ok = jnp.where(even, below >= 0, above < count)
        if 2 * phase == count:
            return [jnp.where(even_ok, at_even, at_odd), even_ok]
        return [at_even, at_odd, even_ok, odd_ok]

    edge = (me == 0) | (me == count - 1)
    plan, places = [block, edge], {}

    def planned(name, values):
        places[name] = len(plan)
        plan.extend(values)

    planned("own", [me, 1])
    for phase in range(1, count - 1):
        planned(("gate", phase), shards(phase))
    planned("first", [shared(1)])
    chunks = []
    for phase in range(2, count):
        if 2 * phase <= count:
            chunks.append(shared(phase))
        else:
            chunks.append(reached(phase, even))
            if phase + 1 < count:
                chunks.append(reached(phase + 1, ~even))
    chunks.append(me)
    planned("chunks", chunks)
    plan = scalars(*plan)

    half = tokens // 2
    evens = [swap_even(grad_out[half:], count)]
    odds = [swap_odd(grad_out[half:], count, blocks)]
    rest, plan, rate, lam, span, res, filters = tie(grad_out, plan, rate, lam, span, res, filters)
    evens.append(swap_even(rest[:half], count))
    odds.append(swap_odd(rest[:half], count, blocks))
    evens[0], odds[0] = tie(evens[0], odds[0])
    acc = None
    for phase in range(1, count - 1):
        ahead = [[swap_even(odds[0], count)], [swap_odd(evens[0], count, blocks)]]
        if phase == 1:
            acc = gate_step(plan, places["own"], None, [[grad_out]], out_weight, 1)
            evens[1], odds[1], acc = tie(evens[1], odds[1], acc)
        ahead[0].append(swap_even(odds[1], count))
        ahead[1].append(swap_odd(evens[1], count, blocks))
        acc = gate_step(
            plan, places["gate", phase], acc, [evens[::-1], odds[::-1]], out_weight,
            1 if 2 * phase == count else 2,
        )
        evens, odds = ahead
        if phase < count - 2:
            evens[0], odds[0], acc = tie(evens[0], odds[0], acc)
            evens[1], odds[1] = tie(evens[1], odds[1])
        if phase == 1:
            odds[0], features, saved_conv = tie(odds[0], features, saved_conv)
            kv_halo = tiles(features[1:3, :extra].astype(f32))
            kv_halo = lax.ppermute(kv_halo, "ctx", [(i, (i - 1) % blocks) for i in range(blocks)])
            last = jnp.where(
                even, jnp.minimum(count - 1, me + count - 1), jnp.maximum(me - count + 1, 0)
            )
            last_weight = lax.dynamic_slice(out_weight, (0, last * width), (width, width))
            query, keys, values, saved, product = spread_acts(features, saved_conv)
            odds[1], kv_halo, last_weight = tie(odds[1], kv_halo, last_weight)
    late_conv, late_query, later, late_products = close_gate(
        plan, 1, acc, evens[0], last_weight, query, saved, lam, extra, residues=res
    )
    early_conv, early_query, packet = close_gate(
        plan, 1, acc, evens[1], last_weight, query, saved, lam, extra, later=later
    )

    other = swap_ctx(packet, 1, blocks)
    chip = fold(plan, packet, other, span)
    arrived = [swap_ctx(chip, 2 * mask, blocks) for mask in range(1, blocks // 2)]
    early_products, gconv, queries = settle(
        later, late_conv, late_query, early_conv, early_query, lam, res, filters, width
    )

    def added(*parts):
        return sum(value.astype(f32) for value in parts if value is not None).astype(bf16)

    def masked(value):
        return None if value is None else jnp.where(edge, jnp.zeros_like(value), value)

    proj, *part, entering = scan_block(
        plan, places["first"], [late_products, early_products, queries, late_query], keys, values,
        lam, rate, res, filters, kv_halo, packet, other, arrived, in_weight, deep, width,
    )
    total, *parts = project(
        plan, places["chunks"], 1, proj, in_weight, deep, [gconv, product, lam, entering]
    )
    for_even, for_odd = {1: part}, {2: part}
    evens, odds = [swap_even(piece, count) for piece in part], [None, None]
    evens[0], proj, total, *parts = tie(
        evens[0], proj, total, *parts
    )
    parts += project(plan, places["chunks"] + 1, len(chunks) - 1, proj, in_weight, deep)
    for phase in range(2, count):
        for_even[phase], parts = parts[:2], parts[2:]
        if 2 * phase <= count:
            for_odd[phase + 1] = for_even[phase]
        elif phase + 1 < count:
            for_odd[phase + 1], parts = parts[:2], parts[2:]
    for phase in range(2, count):
        if phase > 2:
            for piece in range(2):
                evens[piece], odds[piece] = tie(evens[piece], odds[piece])
        if phase == count - 1:
            odds[0], total = tie(odds[0], total)
        for piece in range(2):
            next_even = swap_even(added(for_even[phase][piece], masked(odds[piece])), count)
            odds[piece] = swap_odd(added(for_odd[phase][piece], evens[piece]), count, blocks)
            evens[piece] = next_even
    mask = 1
    while 2 * mask < blocks:
        total = total + swap_ctx(total, mask, blocks)
        mask *= 2
    other = swap_ctx(total, mask, blocks)
    evens[0], odds[0], evens[1], other = tie(evens[0], odds[0], evens[1], other)
    grad_residue = (total + other) / (tokens * blocks)
    grad_input = jnp.concatenate(
        [added(parts[piece], evens[piece], masked(odds[piece])) for piece in range(2)]
    )
    return grad_input, grad_residue


def solution(mesh):
    return jax.shard_map(
        local,
        mesh=mesh,
        in_specs=(
            P(None, "ctx", "chan"),
            P("ctx", "chan"),
            P("ctx", "chan"),
            P("chan", None),
            P(None, None, "chan"),
            P(None, None, "chan"),
            P(None, "chan"),
            P(None, "chan"),
        ),
        out_specs=(P("chan", "ctx"), P(None, "chan")),
        check_vma=False,
    )
```
